256 devices in a mesh: section: 8 (over x, y_hi), head: 32 (over y_lo, z, core).
Axes of the slice: x: 4, y: 4 (y_hi: 2, y_lo: 2; y = y_hi * 2 + y_lo), z: 8, core: 2. Of those that a mesh axis runs over, the one named last changes fastest.
Arguments:
- states: bfloat16 [8192, 6144], P(('section', 'head')), may hold values from -6 to 6
- levels: int32 [8], replicated, may hold values from 0 to 7, as said below
- span_mask: int32 [8, 8], P('section'), may hold values from 0 to 1, as said below
- norm_gain: float32 [8, 6144], replicated, may hold values from 0.5 to 2.5
- out_gate: float32 [8, 6144], replicated, may hold values from 0.5 to 1.5
- w_query: bfloat16 [6144, 4096], P(None, 'head')
- w_key: bfloat16 [6144, 4096], P(None, 'head')
- w_value: bfloat16 [6144, 4096], P(None, 'head'), may hold values from -0.078125 to 0.078125
- w_out: bfloat16 [4096, 6144], P('head'), may hold values from -0.1875 to 0.1875
Outputs:
- next_states: bfloat16 [8192, 6144], P(('section', 'head'))
The draws below stay inside these ranges and needn't reach their ends.
Inputs may be any that keep to these rules, and one draw needn't show every extreme that they name: levels is a permutation of 0 to 7. span_mask[i][j] is 1 exactly when levels[j] <= levels[i].
All inputs are finite; a program needn't handle non-finite values.
Results may differ from the reference program's by a relative error of at most 0.03.
Values may be sent and summed in bfloat16 or wider, within the bound.
No kernel may reach another device: no remote copies, remote signals or barrier semaphores. Data moves between devices by JAX's collectives and lax.ppermute only.
A program may use at most 128 MiB of HBM per device.

```python
import math
import jax
import jax.numpy as jnp
from jax import lax

D = 6144
HD = 128
HEAD_DEV = 1
HEADS = 32
ROWS = 1024
SPANS = 8
TOKENS = 8192
N_HEAD = 32


def shared_order(key):
    return jax.random.permutation(key, SPANS).astype(jnp.int32)


def draw_levels(key, part):
    order = shared_order(key)
    return order


def draw_span_mask(key, part):
    order = shared_order(key)
    return (order[None, :] <= order[:, None]).astype(jnp.int32)


def draw_w_query(key, part):
    key = jax.random.fold_in(key, 3)
    own = jnp.clip(jax.random.normal(key, (D, HEADS * HD), jnp.float32), -6.0, 6.0)
    return (2.5 * own / math.sqrt(D)).astype(jnp.bfloat16)


def draw_w_key(key, part):
    key = jax.random.fold_in(key, 4)
    own = jnp.clip(jax.random.normal(key, (D, HEADS * HD), jnp.float32), -6.0, 6.0)
    return (own / math.sqrt(D)).astype(jnp.bfloat16)


def draw_norm_gain(key, part):
    key = jax.random.fold_in(key, 5)
    second = jax.random.fold_in(key, 1)
    return jax.random.uniform(second, (SPANS, D), jnp.float32, 0.6, 1.4)


def draw_states(key, part):
    key = jax.random.fold_in(key, 6)
    first = jax.random.fold_in(key, 0)
    return jnp.clip(jax.random.normal(first, (TOKENS, D), jnp.float32), -6.0, 6.0).astype(jnp.bfloat16)


def steps_of(key, extent, cuts, smallest, largest):
    loudness, own = 1.0, jax.random.fold_in(key, 6)
    for dim, shards_of in cuts:
        heights = jnp.exp(jax.random.uniform(jax.random.fold_in(own, dim), (shards_of,), jnp.float32, smallest / len(cuts), largest / len(cuts)))
        loudness = loudness * jnp.repeat(heights, extent[dim] // shards_of).reshape([-1 if axis == dim else 1 for axis in range(len(extent))])
    return loudness


def normal_values(key, dims, scale, most, pieces=(), held_as=jnp.bfloat16):
    level = steps_of(key, dims, pieces, -0.22, 0.18) if pieces else 1.0
    entries = jax.random.normal(key, dims, jnp.float32) * scale * level
    return jnp.minimum(jnp.maximum(entries, -most), most).astype(held_as)


def setup_inputs(seed: int = 0) -> dict:
    arg_keys = jax.random.split(jax.random.key(seed), 10)
    states = draw_states(jax.random.fold_in(arg_keys[9], 71), 0)
    levels = draw_levels(jax.random.fold_in(arg_keys[9], 71), 0)
    span_mask = draw_span_mask(jax.random.fold_in(arg_keys[9], 71), 0)
    norm_gain = draw_norm_gain(jax.random.fold_in(arg_keys[9], 71), 0)
    out_gate = jnp.clip(jax.random.uniform(arg_keys[4], (SPANS, D), jnp.float32, 0.5, 1.5), 0.5, 1.5)
    w_query = draw_w_query(jax.random.fold_in(arg_keys[9], 71), 0)
    w_key = draw_w_key(jax.random.fold_in(arg_keys[9], 71), 0)
    w_value = normal_values(arg_keys[7], (D, HEADS * HD), D ** -0.5, 0.078125, ((1, 32),))
    w_out = normal_values(arg_keys[8], (HEADS * HD, D), (HEADS * HD // 4) ** -0.5, 0.1875, ((0, 32),))
    return {"states": states, "levels": levels, "span_mask": span_mask, "norm_gain": norm_gain, "out_gate": out_gate, "w_query": w_query, "w_key": w_key, "w_value": w_value, "w_out": w_out}


def reference(states, levels, span_mask, norm_gain, out_gate, w_query, w_key, w_value, w_out):
    floats = states.astype(jnp.float32).reshape(SPANS, ROWS, D)
    gains = norm_gain[levels]
    normed = floats * lax.rsqrt(lax.optimization_barrier(jnp.mean(floats * floats, axis=-1, keepdims=True)) + 1e-06) * gains[:, None, :]
    normed = normed.astype(jnp.bfloat16).reshape(TOKENS, D)

    def project(weight):
        return jnp.dot(normed, weight, preferred_element_type=jnp.float32).astype(jnp.bfloat16).reshape(TOKENS, HEADS, HD)
    queries = project(w_query)
    keys_all = project(w_key).astype(jnp.float32)
    values_all = project(w_value).astype(jnp.float32)
    key_span = jnp.arange(TOKENS, dtype=jnp.int32) // ROWS

    def one_span(which):
        allowed = span_mask[which][key_span] == 1
        rows_q = lax.dynamic_slice_in_dim(queries, (which * ROWS).astype(jnp.int32), ROWS, 0).astype(jnp.float32)
        scores = jnp.einsum('rhd,khd->rhk', rows_q, keys_all) / math.sqrt(HD)
        scores = jnp.where(allowed[None, None, :], scores, -jnp.inf)
        highest = lax.optimization_barrier(jnp.max(scores, axis=-1, keepdims=True))
        weights = jnp.where(allowed[None, None, :], jnp.exp(scores - highest), 0.0)
        total = lax.optimization_barrier(jnp.sum(weights, axis=-1))
        rounded = lax.optimization_barrier(weights.astype(jnp.bfloat16)).astype(jnp.float32)
        mixed = jnp.einsum('rhk,khd->rhd', rounded, values_all)
        return (mixed / total[..., None]).astype(jnp.bfloat16).reshape(ROWS, HEADS * HD)
    attended = lax.map(one_span, jnp.arange(SPANS, dtype=jnp.int32)).reshape(TOKENS, N_HEAD, HEAD_DEV * HD)
    grouped_out = w_out.reshape(N_HEAD, HEAD_DEV * HD, D)

    def add_group(group, total):
        left = lax.dynamic_index_in_dim(attended, group, 1, keepdims=False)
        right = lax.dynamic_index_in_dim(grouped_out, group, 0, keepdims=False)
        term = jnp.dot(left, right, preferred_element_type=jnp.float32).astype(jnp.bfloat16)
        return total + lax.optimization_barrier(term).astype(jnp.float32)
    proj = lax.fori_loop(0, N_HEAD, add_group, jnp.zeros((TOKENS, D), jnp.float32)).reshape(SPANS, ROWS, D)
    gates = out_gate[levels]
    updated = (floats + gates[:, None, :] * proj).astype(jnp.bfloat16)
    return jnp.roll(updated, 1, axis=0).reshape(TOKENS, D)
```

```python
import functools
import math

import jax
import jax.numpy as jnp
from jax import lax
from jax.experimental import pallas as pl
from jax.experimental.pallas import tpu as pltpu
from jax.sharding import PartitionSpec as P

HD = 128
Z = 8
F32 = jnp.float32
BF16 = jnp.bfloat16
VMEM_LIMIT = 40 * 1024 * 1024
LOW = -3.0e38


def head_of(yl, z, core):
    return (yl * Z + z % Z) * 2 + core


def z_route(step):
    return [
        (head_of(yl, z, c), head_of(yl, z + step, c))
        for yl in range(2)
        for z in range(Z)
        for c in range(2)
    ]


UP, DOWN = z_route(1), z_route(-1)
ACROSS = [(h, h ^ 16) for h in range(32)]
CORE = [(h, h ^ 1) for h in range(32)]


def x_route(step):
    return [(x * 2 + yh, ((x + step) % 4) * 2 + yh) for x in range(4) for yh in range(2)]


XUP, XDOWN = x_route(1), x_route(-1)
YH = [(s, s ^ 1) for s in range(8)]
NEXT = [(s, (s + 1) % 8) for s in range(8)]


def send(value, route):
    return lax.ppermute(value, "head", route)


def send_sec(value, route):
    return lax.ppermute(value, "section", route)


def fence(*values):
    return lax.optimization_barrier(values)


def params(**kw):
    return pltpu.CompilerParams(vmem_limit_bytes=VMEM_LIMIT, **kw)


def fold_kernel(level_ref, gain_ref, *refs):
    ws, out_ref = refs[:-1], refs[-1]
    row = gain_ref[pl.ds(level_ref[0], 1), :]
    for i in range(row.shape[1] // HD):
        rows = slice(i * HD, (i + 1) * HD)
        col = jnp.transpose(jnp.broadcast_to(row[:, rows], (HD, HD)))
        for j, ref in enumerate(ws):
            out_ref[rows, j * HD : (j + 1) * HD] = (ref[rows, :].astype(F32) * col).astype(BF16)


def fold(level, gain, weights):
    d = gain.shape[1]
    steps = 6
    tile = d // steps
    n = len(weights)
    return pl.pallas_call(
        fold_kernel,
        grid=(steps,),
        in_specs=[
            pl.BlockSpec(memory_space=pltpu.SMEM),
            pl.BlockSpec((gain.shape[0], tile), lambda i: (0, i)),
        ]
        + [pl.BlockSpec((tile, HD), lambda i: (i, 0))] * n,
        out_specs=pl.BlockSpec((tile, n * HD), lambda i: (i, 0)),
        out_shape=jax.ShapeDtypeStruct((d, n * HD), BF16),
        compiler_params=params(),
        cost_estimate=pl.CostEstimate(flops=n * d * HD, bytes_accessed=4 * n * d * HD, transcendentals=0),
        name="fold",
    )(level, gain, *weights)


def project_kernel(n, d, *refs):
    xs, (w_ref, own_ref, oth_ref, acc, ss) = refs[:n], refs[n:]
    k = pl.program_id(0)

    @pl.when(k == 0)
    def _():
        acc[...] = jnp.zeros_like(acc)
        ss[...] = jnp.zeros_like(ss)

    x = jnp.concatenate([r[...] for r in xs], axis=0)
    acc[...] += jnp.dot(x, w_ref[...], preferred_element_type=F32)
    part = None
    for i in range(x.shape[1] // HD):
        piece = x[:, i * HD : (i + 1) * HD].astype(F32)
        part = piece * piece if part is None else part + piece * piece
    ss[...] += part

    @pl.when(k == pl.num_programs(0) - 1)
    def _():
        r = lax.rsqrt(jnp.sum(ss[...], axis=1, keepdims=True) / d + 1e-06)
        rq = r * (math.log2(math.e) / math.sqrt(HD))
        for ref, base in ((own_ref, 0), (oth_ref, 3 * HD)):
            ref[:, :HD] = (acc[:, base : base + HD] * rq).astype(BF16)
            ref[:, HD:] = (acc[:, base + HD : base + 3 * HD] * r).astype(BF16)


def project(blocks, w):
    d, cols = w.shape
    rows = sum(b.shape[0] for b in blocks)
    tile = 1024
    xspecs = [pl.BlockSpec((b.shape[0], tile), lambda k: (0, k)) for b in blocks]
    ospec = pl.BlockSpec((rows, cols // 2), lambda k: (0, 0))
    shape = jax.ShapeDtypeStruct((rows, cols // 2), BF16)
    return pl.pallas_call(
        functools.partial(project_kernel, len(blocks), d),
        grid=(d // tile,),
        in_specs=xspecs + [pl.BlockSpec((tile, cols), lambda k: (k, 0))],
        out_specs=[ospec, ospec],
        out_shape=[shape, shape],
        scratch_shapes=[pltpu.VMEM((rows, cols), F32), pltpu.VMEM((rows, HD), F32)],
        compiler_params=params(),
        cost_estimate=pl.CostEstimate(
            flops=2 * rows * d * cols, bytes_accessed=2 * d * (rows + cols), transcendentals=0
        ),
        name="project",
    )(*blocks, w)


def attend_kernel(n, first, last, levels_ref, ids_ref, *refs):
    q_ref, kvs, rest = refs[0], refs[1 : 1 + n], refs[1 + n :]
    if first:
        outs = rest
    else:
        m_in, acc_in, outs = rest[0], rest[1], rest[2:]
    if last:
        out_ref, m, acc = outs
    else:
        m, acc = outs
    if first:
        m[...] = jnp.full_like(m, LOW)
        acc[...] = jnp.zeros_like(acc)
    else:
        m[...] = m_in[...]
        acc[...] = acc_in[...]
    mine = levels_ref[ids_ref[0]]
    for i in range(n):

        @pl.when(levels_ref[ids_ref[1 + i]] <= mine)
        def _(kv=kvs[i]):
            s = lax.dot_general(
                q_ref[...], kv[:, :HD], (((1,), (1,)), ((), ())), preferred_element_type=F32
            )
            old = m[...]
            new = jnp.maximum(old, jnp.max(s, axis=1, keepdims=True))
            p = jnp.exp2(s - new[:, :1]).astype(BF16)
            v = jnp.concatenate([kv[:, HD:], jnp.ones((kv.shape[0], HD), BF16)], axis=1)
            added = jnp.dot(p, v, preferred_element_type=F32)
            scale = jnp.exp2(old - new)
            acc[...] = acc[...] * jnp.concatenate([scale, scale], axis=1) + added
            m[...] = new

    if last:
        out_ref[...] = (acc[:, :HD] / acc[:, HD:]).astype(BF16)


def attend(levels, ids, q, kvs, state, last):
    rows = q.shape[0]
    tile = 256
    n = len(kvs)
    first = state is None
    smem = pl.BlockSpec(memory_space=pltpu.SMEM)
    qspec = pl.BlockSpec((tile, HD), lambda i: (i, 0))
    aspec = pl.BlockSpec((tile, 2 * HD), lambda i: (i, 0))
    in_specs = [smem, smem, qspec] + [pl.BlockSpec(kv.shape, lambda i: (0, 0)) for kv in kvs]
    if not first:
        in_specs += [qspec, aspec]
    if last:
        out_specs = qspec
        out_shape = jax.ShapeDtypeStruct((rows, HD), BF16)
        scratch = [pltpu.VMEM((tile, HD), F32), pltpu.VMEM((tile, 2 * HD), F32)]
    else:
        out_specs = [qspec, aspec]
        out_shape = [
            jax.ShapeDtypeStruct((rows, HD), F32),
            jax.ShapeDtypeStruct((rows, 2 * HD), F32),
        ]
        scratch = []
    return pl.pallas_call(
        functools.partial(attend_kernel, n, first, last),
        grid=(rows // tile,),
        in_specs=in_specs,
        out_specs=out_specs,
        out_shape=out_shape,
        scratch_shapes=scratch,
        compiler_params=params(),
        cost_estimate=pl.CostEstimate(
            flops=sum(8 * rows * kv.shape[0] * HD for kv in kvs),
            bytes_accessed=4 * rows * HD * 8,
            transcendentals=sum(rows * kv.shape[0] for kv in kvs),
        ),
        name="attend",
    )(levels, ids, q, *kvs, *(() if first else state))


def partial_kernel(own_at, oth_at, labels, att_ref, part_ref, w_ref, *outs):
    size = 32
    count = labels * size
    mine = jnp.concatenate([att_ref[own_at : own_at + count], att_ref[oth_at : oth_at + count]], axis=0)
    other = jnp.concatenate([part_ref[oth_at : oth_at + count], part_ref[own_at : own_at + count]], axis=0)
    a = jnp.concatenate([mine, other], axis=1)
    step = 512
    for j in range(0, w_ref.shape[1], step):
        r = jnp.dot(a, w_ref[:, j : j + step], preferred_element_type=F32).astype(BF16)
        for o, ref in enumerate(outs):
            ref[:, j : j + step] = r[o * size : (o + 1) * size]


def partials(att, partner, w, own_at, oth_at, labels):
    cols = w.shape[1]
    vm = pl.BlockSpec(memory_space=pltpu.VMEM)
    outs = pl.pallas_call(
        functools.partial(partial_kernel, own_at, oth_at, labels),
        in_specs=[vm, vm, vm],
        out_specs=[vm] * (2 * labels),
        out_shape=[jax.ShapeDtypeStruct((32, cols), BF16)] * (2 * labels),
        compiler_params=params(),
        cost_estimate=pl.CostEstimate(
            flops=2 * 64 * labels * 2 * HD * cols, bytes_accessed=2 * cols * (64 * labels + 2 * HD), transcendentals=0
        ),
        name="partials",
    )(att, partner, w)
    return outs[:labels], outs[labels:]


def plus(*terms):
    total = terms[0].astype(F32)
    for t in terms[1:]:
        total = total + t.astype(F32)
    return total.astype(BF16)


ROUNDS = (
    (("ma", "m0", UP), ("mb", "m0", DOWN), ("n0", "m0", ACROSS)),
    (("ma2", "ma", UP), ("mb2", "mb", DOWN), ("na1", "ma", ACROSS)),
    (("ma3", "ma2", UP), ("mb3", "mb2", DOWN), ("nb1", "mb", ACROSS)),
    (("na2", "na1", UP), ("nb2", "nb1", DOWN), ("na3", "ma3", ACROSS)),
    (("n4", "na3", UP), ("m4", "mb3", DOWN), ("nb3", "mb3", ACROSS)),
)
GROUP_A = ("m0", "ma", "mb", "n0", "ma2", "mb2", "na1", "ma3")
GROUP_B = ("mb3", "nb1", "na2", "nb2")
GROUP_C = ("na3", "n4", "m4", "nb3")


def back(route):
    return [(j, i) for i, j in route]


def gather_round(held, number, extras=()):
    new = {name: send(held[source], route) for name, source, route in ROUNDS[number]}
    return fence({**held, **new}, extras)


def reduce_rounds(held):
    held = dict(held)
    for entries in ROUNDS[::-1]:
        got = fence(*[send(held[name], back(route)) for name, _, route in entries])
        for target in dict.fromkeys(source for _, source, _ in entries):
            held[target] = plus(held[target], *[g for g, e in zip(got, entries) if e[1] == target])
    return held["m0"]


def shards(states, levels, span_mask, norm_gain, out_gate, w_query, w_key, w_value, w_out):
    half = w_out.shape[1] // 2
    own_weights = (w_query, w_key, w_value)

    first = {"m0": states[:16]}
    second = {"m0": states[16:]}
    first, _ = gather_round(first, 0)
    oth_weights = tuple(send(w, CORE) for w in own_weights)
    second, (oth_weights, levels) = gather_round(second, 0, (oth_weights, levels))

    sec = lax.axis_index("section")
    core = lax.axis_index("head") % 2
    x, yh = sec // 2, sec % 2
    before = (sec + 7) % 8

    def sid(dx, flip):
        return ((x + dx) % 4) * 2 + (yh ^ flip)

    def ids(*which):
        return jnp.stack([before, *which])

    first, _ = gather_round(first, 1)
    w = fold(levels[sec].reshape(1), norm_gain, own_weights + oth_weights)
    second, (w, states, w_out) = gather_round(second, 1, (w, states, w_out))

    first, _ = gather_round(first, 2)
    old = send_sec(states, NEXT)
    out_mine = lax.dynamic_slice_in_dim(w_out, core * half, half, 1)
    out_theirs = send(lax.dynamic_slice_in_dim(w_out, (1 - core) * half, half, 1), CORE)
    second, (w, old, out_mine, out_theirs) = gather_round(second, 2, (w, old, out_mine, out_theirs))

    def rows_of(names):
        return [held[name] for name in names for held in (first, second)]

    def columns(pair):
        return [p[:, :HD] for p in pair], [p[:, HD:] for p in pair]

    group_a = rows_of(GROUP_A)
    first, _ = gather_round(first, 3)
    mine, theirs = project(group_a, w)
    second, (w, mine, theirs) = gather_round(second, 3, (w, mine, theirs))
    group_b = rows_of(GROUP_B)

    first, _ = gather_round(first, 4)
    q_a, kv_a = columns((mine, send(theirs, CORE)))
    kv_a = jnp.concatenate(kv_a, axis=0)
    q_a = send_sec(jnp.concatenate(q_a, axis=0), NEXT)
    mine, theirs = project(group_b, w)
    second, (w, mine, theirs) = gather_round(second, 4, (w, mine, theirs))
    q_b, kv_b = columns((mine, send(theirs, CORE)))
    mine, theirs = project(rows_of(GROUP_C), w)
    q_c, kv_c = columns((mine, send(theirs, CORE)))
    kv_b = jnp.concatenate(kv_b + kv_c, axis=0)
    q_b = send_sec(jnp.concatenate(q_b + q_c, axis=0), NEXT)

    def spread(kv):
        a, b, p = fence(send_sec(kv, XUP), send_sec(kv, XDOWN), send_sec(kv, YH))
        c, pa, pb = fence(send_sec(a, XUP), send_sec(a, YH), send_sec(p, XDOWN))
        cut = kv.shape[0] // 2
        pc = [send_sec(pa[:cut], XUP), send_sec(pb[cut:], XDOWN)]
        return (a, b, p), (c, pa, pb), pc

    near = (sec, sid(-1, 0), sid(1, 0), sid(0, 1))
    mid = (sid(2, 0), sid(-1, 1), sid(1, 1))
    far = (sid(2, 1), sid(2, 1))
    one, two, three = spread(kv_a)
    one_b, two_b, three_b = spread(kv_b)
    q = jnp.concatenate([q_a, q_b], axis=0)
    state = attend(levels, ids(*near), q, [kv_a, *one], None, False)
    state = attend(levels, ids(*mid, *far), q, [*two, *three], state, False)
    state = attend(levels, ids(*near), q, [kv_b, *one_b], state, False)
    state = attend(levels, ids(*mid), q, [*two_b], state, False)
    att = attend(levels, ids(*far), q, three_b, state, True)

    w_both = jnp.concatenate([out_mine, out_theirs], axis=0)
    partner = send(att, CORE)
    sums = ({}, {})
    for names, own_at, oth_at in ((GROUP_C, 768, 896), (GROUP_B, 512, 640), (GROUP_A, 0, 256)):
        for held, made in zip(sums, partials(att, partner, w_both, own_at, oth_at, len(names))):
            held.update(zip(names, made))
    mine, theirs = [reduce_rounds(held) for held in sums]
    got = send(theirs, CORE)
    lo = jnp.where(core == 0, mine, got)
    hi = jnp.where(core == 0, got, mine)
    proj = jnp.concatenate([lo, hi], axis=1).astype(F32)
    gate = lax.dynamic_index_in_dim(out_gate, levels[before], 0, keepdims=True)
    return (old.astype(F32) + gate * proj).astype(BF16)


def solution(mesh):
    return jax.shard_map(
        shards,
        mesh=mesh,
        in_specs=(
            P(("section", "head"), None),
            P(),
            P("section", None),
            P(),
            P(),
            P(None, "head"),
            P(None, "head"),
            P(None, "head"),
            P("head", None),
        ),
        out_specs=P(("section", "head"), None),
        check_vma=False,
    )
```

```python
import functools
import math

import jax
import jax.numpy as jnp
from jax import lax
from jax.experimental import pallas as pl
from jax.experimental.pallas import tpu as pltpu
from jax.sharding import PartitionSpec as P

HD = 128
Z = 8
F32 = jnp.float32
BF16 = jnp.bfloat16
VMEM_LIMIT = 24 * 1024 * 1024
LOW = -3.0e38


def head_of(yl, z, core):
    return (yl * Z + z % Z) * 2 + core


def z_route(step):
    return [
        (head_of(yl, z, c), head_of(yl, z + step, c))
        for yl in range(2)
        for z in range(Z)
        for c in range(2)
    ]


AWAY = [r for r in z_route(1) if r[0] % 2 == 0] + [r for r in z_route(-1) if r[0] % 2 == 1]
HOME = [(j, i) for i, j in AWAY]
ACROSS = [(h, h ^ 16) for h in range(32)]
CORE = [(h, h ^ 1) for h in range(32)]


def x_route(step):
    return [(x * 2 + yh, ((x + step) % 4) * 2 + yh) for x in range(4) for yh in range(2)]


XUP, XDOWN = x_route(1), x_route(-1)
YH = [(s, s ^ 1) for s in range(8)]
NEXT = [(s, (s + 1) % 8) for s in range(8)]


def send(value, route):
    return lax.ppermute(value, "head", route)


def send_sec(value, route):
    return lax.ppermute(value, "section", route)


def fence(*values):
    return lax.optimization_barrier(values)


def params(**kw):
    return pltpu.CompilerParams(vmem_limit_bytes=VMEM_LIMIT, **kw)


def pack_kernel(*refs):
    ws, (out_ref, mark_ref) = refs[:-2], refs[-2:]
    for j, ref in enumerate(ws):
        out_ref[:, j * HD : (j + 1) * HD] = ref[...]
    mark_ref[...] = jnp.zeros_like(mark_ref)


def pack(weights):
    d = weights[0].shape[0]
    n = len(weights)
    tile = d // 6
    return pl.pallas_call(
        pack_kernel,
        grid=(6,),
        in_specs=[pl.BlockSpec((tile, HD), lambda i: (i, 0))] * n,
        out_specs=[
            pl.BlockSpec((tile, n * HD), lambda i: (i, 0)),
            pl.BlockSpec((8, HD), lambda i: (0, 0)),
        ],
        out_shape=[pltpu.VMEM((d, n * HD), BF16), jax.ShapeDtypeStruct((8, HD), F32)],
        compiler_params=params(),
        cost_estimate=pl.CostEstimate(flops=0, bytes_accessed=4 * n * d * HD, transcendentals=0),
        name="pack",
    )(*weights)


def project_kernel(n, d, level_ref, gain_ref, *refs):
    xs, (w_ref, own_ref, oth_ref, acc, ss) = refs[:n], refs[n:]
    k = pl.program_id(0)

    @pl.when(k == 0)
    def _():
        acc[...] = jnp.zeros_like(acc)
        ss[...] = jnp.zeros_like(ss)

    gain = gain_ref[pl.ds(level_ref[0], 1), :]
    x = jnp.concatenate([r[...] for r in xs], axis=0)
    part, scaled = None, []
    for i in range(x.shape[1] // HD):
        piece = x[:, i * HD : (i + 1) * HD].astype(F32)
        part = piece * piece if part is None else part + piece * piece
        scaled.append((piece * gain[:, i * HD : (i + 1) * HD]).astype(BF16))
    ss[...] += part
    acc[...] += jnp.dot(jnp.concatenate(scaled, axis=1), w_ref[...], preferred_element_type=F32)

    @pl.when(k == pl.num_programs(0) - 1)
    def _():
        r = lax.rsqrt(jnp.sum(ss[...], axis=1, keepdims=True) / d + 1e-06)
        rq = r * (math.log2(math.e) / math.sqrt(HD))
        for ref, base in ((own_ref, 0), (oth_ref, 3 * HD)):
            ref[:, :HD] = (acc[:, base : base + HD] * rq).astype(BF16)
            ref[:, HD:] = (acc[:, base + HD : base + 3 * HD] * r).astype(BF16)


def project(level, gain, blocks, w):
    d, cols = w.shape
    rows = sum(b.shape[0] for b in blocks)
    tile = 1024
    xspecs = [pl.BlockSpec((b.shape[0], tile), lambda k: (0, k)) for b in blocks]
    ospec = pl.BlockSpec((rows, cols // 2), lambda k: (0, 0))
    shape = jax.ShapeDtypeStruct((rows, cols // 2), BF16)
    return pl.pallas_call(
        functools.partial(project_kernel, len(blocks), d),
        grid=(d // tile,),
        in_specs=[
            pl.BlockSpec(memory_space=pltpu.SMEM),
            pl.BlockSpec((gain.shape[0], tile), lambda k: (0, k)),
            *xspecs,
            pl.BlockSpec((tile, cols), lambda k: (k, 0)),
        ],
        out_specs=[ospec, ospec],
        out_shape=[shape, shape],
        scratch_shapes=[pltpu.VMEM((rows, cols), F32), pltpu.VMEM((rows, HD), F32)],
        compiler_params=params(),
        cost_estimate=pl.CostEstimate(
            flops=2 * rows * d * cols, bytes_accessed=2 * d * (rows + cols), transcendentals=0
        ),
        name="project",
    )(level, gain, *blocks, w)


def attend_kernel(n, first, last, levels_ref, ids_ref, *refs):
    q_ref, kvs, rest = refs[0], refs[1 : 1 + n], refs[1 + n :]
    if first:
        outs = rest
    else:
        m_in, acc_in, outs = rest[0], rest[1], rest[2:]
    if last:
        out_ref, m, acc = outs
    else:
        m, acc = outs
    if first:
        m[...] = jnp.full_like(m, LOW)
        acc[...] = jnp.zeros_like(acc)
    else:
        m[...] = m_in[...]
        acc[...] = acc_in[...]
    mine = levels_ref[ids_ref[0]]
    sub = 128
    for i in range(n):

        @pl.when(levels_ref[ids_ref[1 + i]] <= mine)
        def _(kv=kvs[i]):
            k = kv[:, :HD]
            v = jnp.concatenate([kv[:, HD:], jnp.ones((kv.shape[0], HD), BF16)], axis=1)
            for at in range(0, q_ref.shape[0], sub):
                rows = slice(at, at + sub)
                s = lax.dot_general(
                    q_ref[rows, :], k, (((1,), (1,)), ((), ())), preferred_element_type=F32
                )
                old = m[rows, :]
                new = jnp.maximum(old, jnp.max(s, axis=1, keepdims=True))
                p = jnp.exp2(s - new[:, :1]).astype(BF16)
                added = jnp.dot(p, v, preferred_element_type=F32)
                scale = jnp.exp2(old - new)
                acc[rows, :] = acc[rows, :] * jnp.concatenate([scale, scale], axis=1) + added
                m[rows, :] = new

    if last:
        out_ref[...] = (acc[:, :HD] / acc[:, HD:]).astype(BF16)


def attend(levels, ids, q, kvs, state, last):
    rows = q.shape[0]
    tile = rows
    n = len(kvs)
    first = state is None
    smem = pl.BlockSpec(memory_space=pltpu.SMEM)
    qspec = pl.BlockSpec((tile, HD), lambda i: (i, 0))
    aspec = pl.BlockSpec((tile, 2 * HD), lambda i: (i, 0))
    in_specs = [smem, smem, qspec] + [pl.BlockSpec(kv.shape, lambda i: (0, 0)) for kv in kvs]
    if not first:
        in_specs += [qspec, aspec]
    if last:
        out_specs = qspec
        out_shape = jax.ShapeDtypeStruct((rows, HD), BF16)
        scratch = [pltpu.VMEM((tile, HD), F32), pltpu.VMEM((tile, 2 * HD), F32)]
    else:
        out_specs = [qspec, aspec]
        out_shape = [
            jax.ShapeDtypeStruct((rows, HD), F32),
            jax.ShapeDtypeStruct((rows, 2 * HD), F32),
        ]
        scratch = []
    return pl.pallas_call(
        functools.partial(attend_kernel, n, first, last),
        grid=(rows // tile,),
        in_specs=in_specs,
        out_specs=out_specs,
        out_shape=out_shape,
        scratch_shapes=scratch,
        compiler_params=params(),
        cost_estimate=pl.CostEstimate(
            flops=sum(8 * rows * kv.shape[0] * HD for kv in kvs),
            bytes_accessed=4 * rows * HD * 8,
            transcendentals=sum(rows * kv.shape[0] for kv in kvs),
        ),
        name="attend",
    )(levels, ids, q, *kvs, *(() if first else state))


def partial_kernel(start, sizes, att_ref, partner_ref, w_ref, *outs):
    rows = slice(start, start + sum(sizes))
    a = jnp.concatenate([att_ref[rows, :], partner_ref[rows, :]], axis=1)
    step = 512
    for j in range(0, w_ref.shape[1], step):
        r = jnp.dot(a, w_ref[:, j : j + step], preferred_element_type=F32).astype(BF16)
        at = 0
        for size, ref in zip(sizes, outs):
            ref[:, j : j + step] = r[at : at + size]
            at += size


def partials(att, partner, w, start, sizes):
    rows, cols = sum(sizes), w.shape[1]
    vm = pl.BlockSpec(memory_space=pltpu.VMEM)
    return pl.pallas_call(
        functools.partial(partial_kernel, start, sizes),
        in_specs=[vm, vm, vm],
        out_specs=[vm] * len(sizes),
        out_shape=[jax.ShapeDtypeStruct((n, cols), BF16) for n in sizes],
        compiler_params=params(),
        cost_estimate=pl.CostEstimate(
            flops=4 * rows * HD * cols, bytes_accessed=2 * cols * (rows + 2 * HD), transcendentals=0
        ),
        name="partials",
    )(att, partner, w)


def plus(*terms):
    total = terms[0].astype(F32)
    for t in terms[1:]:
        total = total + t.astype(F32)
    return total.astype(BF16)


SETS = ((32, 64, 64, 64, 32, 64), (64, 32), (64, 32))


def shards(states, levels, span_mask, norm_gain, out_gate, w_query, w_key, w_value, w_out):
    n = states.shape[0]
    own_weights = (w_query, w_key, w_value)

    chip = jnp.concatenate([states, send(states, CORE)], axis=0)
    f1, g0 = send(chip, AWAY), send(states, ACROSS)
    oth_weights = tuple(send(w, CORE) for w in own_weights)
    f1, g0, oth_weights, levels, w_out, old = fence(f1, g0, oth_weights, levels, w_out, states)

    sec = lax.axis_index("section")
    x, yh = sec // 2, sec % 2
    before = (sec + 7) % 8

    def sid(dx, flip):
        return ((x + dx) % 4) * 2 + (yh ^ flip)

    def ids(*which):
        return jnp.stack([before, *which])

    f2, g1a = send(f1, AWAY), send(f1[:n], ACROSS)
    w, mark = pack(own_weights + oth_weights)
    old = send_sec(old, NEXT)
    f2, g1a, mark, w_out, old, f1 = fence(f2, g1a, mark, w_out, old, f1)

    f3, g1b = send(f2, AWAY), send(f1[n:], ACROSS)
    w_both = jnp.concatenate([w_out, send(w_out, CORE)], axis=0)
    level = levels[sec].reshape(1)
    f3, g1a, g1b, w_both, level, f1, f2 = fence(f3, g1a, g1b, w_both, level, f1, f2)
    g1 = jnp.concatenate([g1a, g1b], axis=0)

    g2, g3a = send(g1, AWAY), send(f3[:n], ACROSS)
    own1, oth1 = project(level, norm_gain, [states, f1, f2, f3, g0, g1], w)
    g2, g3a, f3, own1, oth1 = fence(g2, g3a, f3, own1, oth1)

    h, g3b = send(jnp.concatenate([f3[:n], g3a], axis=0), AWAY), send(f3[n:], ACROSS)
    oth1 = send(oth1, CORE)
    own2, oth2 = project(level, norm_gain, [g2, g3a], w)
    h, g3b, oth1, own2, oth2 = fence(h, g3b, oth1, own2, oth2)
    oth2 = send(oth2, CORE)
    own3, oth3 = project(level, norm_gain, [h, g3b], w)
    oth3 = send(oth3, CORE)

    mine = (own1, own2, own3, oth1, oth2, oth3)
    kv = jnp.concatenate([p[:, HD:] for p in mine], axis=0)
    q = jnp.concatenate([p[:, :HD] for p in mine], axis=0)
    a, b, p, q = fence(send_sec(kv, XUP), send_sec(kv, XDOWN), send_sec(kv, YH), send_sec(q, NEXT))
    c, pa, pb = send_sec(a, XUP), send_sec(a, YH), send_sec(p, XDOWN)
    near = ids(sec, sid(-1, 0), sid(1, 0), sid(0, 1))
    state = attend(levels, near, q, [kv, a, b, p], None, False)
    c, pa, pb, state = fence(c, pa, pb, state)
    cut = kv.shape[0] // 2
    d = [send_sec(pa[:cut], XUP), send_sec(pb[cut:], XDOWN)]
    state = attend(levels, ids(sid(2, 0), sid(-1, 1), sid(1, 1)), q, [c, pa, pb], state, False)
    d, state = fence(d, state)
    att = attend(levels, ids(sid(2, 1), sid(2, 1)), q, d, state, True)

    count = att.shape[0] // 2
    partner = send(att[count:], CORE)
    ends = [sum(SETS[0]), sum(SETS[0]) + sum(SETS[1]), count]
    p3 = partials(att, partner, w_both, ends[1], SETS[2])
    p2 = partials(att, partner, w_both, ends[0], SETS[1])
    p1 = partials(att, partner, w_both, 0, SETS[0])
    m, f1, f2, f3, g0, g1 = p1
    g2, g3a = p2
    h, g3b = p3

    h, g3b = fence(send(h, HOME), send(g3b, ACROSS))
    g2, g3a = fence(send(g2, HOME), send(plus(g3a, h[n:]), ACROSS))
    g1 = plus(g1, g2)
    f3 = jnp.concatenate([plus(f3[:n], h[:n], g3a), plus(f3[n:], g3b)], axis=0)
    g1 = send(g1, ACROSS)
    f3, g0, m = fence(send(f3, HOME), g0, m)
    f2 = plus(f2, f3)
    f2, g1 = fence(send(f2, HOME), g1)
    f1, g0 = fence(send(plus(f1, f2, g1), HOME), send(g0, ACROSS))
    proj = m.astype(F32) + f1[:n].astype(F32) + g0.astype(F32) + send(f1[n:], CORE).astype(F32)
    gate = lax.dynamic_index_in_dim(out_gate, levels[before], 0, keepdims=True)
    return (old.astype(F32) + gate * proj).astype(BF16)


def solution(mesh):
    return jax.shard_map(
        shards,
        mesh=mesh,
        in_specs=(
            P(("section", "head"), None),
            P(),
            P("section", None),
            P(),
            P(),
            P(None, "head"),
            P(None, "head"),
            P(None, "head"),
            P("head", None),
        ),
        out_specs=P(("section", "head"), None),
        check_vma=False,
    )
```

```python
import functools
import math

import jax
import jax.numpy as jnp
from jax import lax
from jax.experimental import pallas as pl
from jax.experimental.pallas import tpu as pltpu
from jax.sharding import PartitionSpec as P

HD = 128
Z = 8
F32 = jnp.float32
BF16 = jnp.bfloat16
VMEM_LIMIT = 24 * 1024 * 1024
LOW = -3.0e38


def head_of(yl, z, core):
    return (yl * Z + z % Z) * 2 + core


def z_route(step):
    return [
        (head_of(yl, z, c), head_of(yl, z + step, c))
        for yl in range(2)
        for z in range(Z)
        for c in range(2)
    ]


AWAY = [r for r in z_route(1) if r[0] % 2 == 0] + [r for r in z_route(-1) if r[0] % 2 == 1]
HOME = [(j, i) for i, j in AWAY]
ACROSS = [(h, h ^ 16) for h in range(32)]
CORE = [(h, h ^ 1) for h in range(32)]


def x_route(step):
    return [(x * 2 + yh, ((x + step) % 4) * 2 + yh) for x in range(4) for yh in range(2)]


XUP, XDOWN = x_route(1), x_route(-1)
YH = [(s, s ^ 1) for s in range(8)]
NEXT = [(s, (s + 1) % 8) for s in range(8)]


def send(value, route):
    return lax.ppermute(value, "head", route)


def send_sec(value, route):
    return lax.ppermute(value, "section", route)


def fence(*values):
    return lax.optimization_barrier(values)


def params(**kw):
    return pltpu.CompilerParams(vmem_limit_bytes=VMEM_LIMIT, **kw)


def pack_kernel(*refs):
    ws, (out_ref, mark_ref) = refs[:-2], refs[-2:]
    for j, ref in enumerate(ws):
        out_ref[:, j * HD : (j + 1) * HD] = ref[...]
    mark_ref[...] = jnp.zeros_like(mark_ref)


def pack(weights):
    d = weights[0].shape[0]
    n = len(weights)
    tile = d // 6
    return pl.pallas_call(
        pack_kernel,
        grid=(6,),
        in_specs=[pl.BlockSpec((tile, HD), lambda i: (i, 0))] * n,
        out_specs=[
            pl.BlockSpec((tile, n * HD), lambda i: (i, 0)),
            pl.BlockSpec((8, HD), lambda i: (0, 0)),
        ],
        out_shape=[pltpu.VMEM((d, n * HD), BF16), jax.ShapeDtypeStruct((8, HD), F32)],
        compiler_params=params(),
        cost_estimate=pl.CostEstimate(flops=0, bytes_accessed=4 * n * d * HD, transcendentals=0),
        name="pack",
    )(*weights)


def project_kernel(n, d, level_ref, gain_ref, *refs):
    xs, (w_ref, own_ref, oth_ref, acc, ss) = refs[:n], refs[n:]
    k = pl.program_id(0)

    @pl.when(k == 0)
    def _():
        acc[...] = jnp.zeros_like(acc)
        ss[...] = jnp.zeros_like(ss)

    gain = gain_ref[pl.ds(level_ref[0], 1), :]
    x = jnp.concatenate([r[...] for r in xs], axis=0)
    part, scaled = None, []
    for i in range(x.shape[1] // HD):
        piece = x[:, i * HD : (i + 1) * HD].astype(F32)
        part = piece * piece if part is None else part + piece * piece
        scaled.append((piece * gain[:, i * HD : (i + 1) * HD]).astype(BF16))
    ss[...] += part
    acc[...] += jnp.dot(jnp.concatenate(scaled, axis=1), w_ref[...], preferred_element_type=F32)

    @pl.when(k == pl.num_programs(0) - 1)
    def _():
        r = lax.rsqrt(jnp.sum(ss[...], axis=1, keepdims=True) / d + 1e-06)
        rq = r * (math.log2(math.e) / math.sqrt(HD))
        for ref, base in ((own_ref, 0), (oth_ref, 3 * HD)):
            ref[:, :HD] = (acc[:, base : base + HD] * rq).astype(BF16)
            ref[:, HD:] = (acc[:, base + HD : base + 3 * HD] * r).astype(BF16)


def project(level, gain, blocks, w):
    d, cols = w.shape
    rows = sum(b.shape[0] for b in blocks)
    tile = 1024
    xspecs = [pl.BlockSpec((b.shape[0], tile), lambda k: (0, k)) for b in blocks]
    ospec = pl.BlockSpec((rows, cols // 2), lambda k: (0, 0))
    shape = jax.ShapeDtypeStruct((rows, cols // 2), BF16)
    return pl.pallas_call(
        functools.partial(project_kernel, len(blocks), d),
        grid=(d // tile,),
        in_specs=[
            pl.BlockSpec(memory_space=pltpu.SMEM),
            pl.BlockSpec((gain.shape[0], tile), lambda k: (0, k)),
            *xspecs,
            pl.BlockSpec((tile, cols), lambda k: (k, 0)),
        ],
        out_specs=[ospec, ospec],
        out_shape=[shape, shape],
        scratch_shapes=[pltpu.VMEM((rows, cols), F32), pltpu.VMEM((rows, HD), F32)],
        compiler_params=params(),
        cost_estimate=pl.CostEstimate(
            flops=2 * rows * d * cols, bytes_accessed=2 * d * (rows + cols), transcendentals=0
        ),
        name="project",
    )(level, gain, *blocks, w)


def join_kernel(columns, *refs):
    ins, outs = refs[: -len(columns)], refs[-len(columns) :]
    for ref, (first, lo, hi) in zip(outs, columns):
        at = 0
        for part in ins[first:]:
            rows = part.shape[0]
            ref[at : at + rows, :] = part[:, lo:hi]
            at += rows


def join(parts, columns):
    vm = pl.BlockSpec(memory_space=pltpu.VMEM)
    return pl.pallas_call(
        functools.partial(join_kernel, columns),
        in_specs=[vm] * len(parts),
        out_specs=[vm] * len(columns),
        out_shape=[
            jax.ShapeDtypeStruct((sum(p.shape[0] for p in parts[first:]), hi - lo), BF16)
            for first, lo, hi in columns
        ],
        compiler_params=params(),
        cost_estimate=pl.CostEstimate(flops=0, bytes_accessed=2000000, transcendentals=0),
        name="join",
    )(*parts)


def attend_kernel(n, first, last, levels_ref, ids_ref, *refs):
    q_ref, kvs, rest = refs[0], refs[1 : 1 + n], refs[1 + n :]
    if first:
        outs = rest
    else:
        m_in, acc_in, outs = rest[0], rest[1], rest[2:]
    if last:
        out_ref, m, acc = outs
    else:
        m, acc = outs
    if first:
        m[...] = jnp.full_like(m, LOW)
        acc[...] = jnp.zeros_like(acc)
    else:
        m[...] = m_in[...]
        acc[...] = acc_in[...]
    mine = levels_ref[ids_ref[0]]
    sub = 128
    for i in range(n):

        @pl.when(levels_ref[ids_ref[1 + i]] <= mine)
        def _(kv=kvs[i]):
            k = kv[:, :HD]
            v = jnp.concatenate([kv[:, HD:], jnp.ones((kv.shape[0], HD), BF16)], axis=1)
            for at in range(0, q_ref.shape[0], sub):
                rows = slice(at, at + sub)
                s = lax.dot_general(
                    q_ref[rows, :], k, (((1,), (1,)), ((), ())), preferred_element_type=F32
                )
                old = m[rows, :]
                new = jnp.maximum(old, jnp.max(s, axis=1, keepdims=True))
                p = jnp.exp2(s - new[:, :1]).astype(BF16)
                added = jnp.dot(p, v, preferred_element_type=F32)
                scale = jnp.exp2(old - new)
                acc[rows, :] = acc[rows, :] * jnp.concatenate([scale, scale], axis=1) + added
                m[rows, :] = new

    if last:
        out_ref[...] = (acc[:, :HD] / acc[:, HD:]).astype(BF16)


def attend(levels, ids, q, kvs, state, last):
    rows = q.shape[0]
    tile = rows
    n = len(kvs)
    first = state is None
    smem = pl.BlockSpec(memory_space=pltpu.SMEM)
    qspec = pl.BlockSpec((tile, HD), lambda i: (i, 0))
    aspec = pl.BlockSpec((tile, 2 * HD), lambda i: (i, 0))
    in_specs = [smem, smem, qspec] + [pl.BlockSpec(kv.shape, lambda i: (0, 0)) for kv in kvs]
    if not first:
        in_specs += [qspec, aspec]
    if last:
        out_specs = qspec
        out_shape = jax.ShapeDtypeStruct((rows, HD), BF16)
        scratch = [pltpu.VMEM((tile, HD), F32), pltpu.VMEM((tile, 2 * HD), F32)]
    else:
        out_specs = [qspec, aspec]
        out_shape = [
            jax.ShapeDtypeStruct((rows, HD), F32),
            jax.ShapeDtypeStruct((rows, 2 * HD), F32),
        ]
        scratch = []
    return pl.pallas_call(
        functools.partial(attend_kernel, n, first, last),
        grid=(rows // tile,),
        in_specs=in_specs,
        out_specs=out_specs,
        out_shape=out_shape,
        scratch_shapes=scratch,
        compiler_params=params(),
        cost_estimate=pl.CostEstimate(
            flops=sum(8 * rows * kv.shape[0] * HD for kv in kvs),
            bytes_accessed=4 * rows * HD * 8,
            transcendentals=sum(rows * kv.shape[0] for kv in kvs),
        ),
        name="attend",
    )(levels, ids, q, *kvs, *(() if first else state))


def partial_kernel(start, sizes, att_ref, partner_ref, w_ref, *outs):
    rows = slice(start, start + sum(sizes))
    a = jnp.concatenate([att_ref[rows, :], partner_ref[rows, :]], axis=1)
    step = 512
    for j in range(0, w_ref.shape[1], step):
        r = jnp.dot(a, w_ref[:, j : j + step], preferred_element_type=F32).astype(BF16)
        at = 0
        for size, ref in zip(sizes, outs):
            ref[:, j : j + step] = r[at : at + size]
            at += size


def partials(att, partner, w, start, sizes):
    rows, cols = sum(sizes), w.shape[1]
    vm = pl.BlockSpec(memory_space=pltpu.VMEM)
    return pl.pallas_call(
        functools.partial(partial_kernel, start, sizes),
        in_specs=[vm, vm, vm],
        out_specs=[vm] * len(sizes),
        out_shape=[jax.ShapeDtypeStruct((n, cols), BF16) for n in sizes],
        compiler_params=params(),
        cost_estimate=pl.CostEstimate(
            flops=4 * rows * HD * cols, bytes_accessed=2 * cols * (rows + 2 * HD), transcendentals=0
        ),
        name="partials",
    )(att, partner, w)


def plus(*terms):
    total = terms[0].astype(F32)
    for t in terms[1:]:
        total = total + t.astype(F32)
    return total.astype(BF16)


SETS = ((32, 64, 64, 64, 32, 64), (64, 32), (64, 32))


def shards(states, levels, span_mask, norm_gain, out_gate, w_query, w_key, w_value, w_out):
    n = states.shape[0]
    own_weights = (w_query, w_key, w_value)

    states = send_sec(states, NEXT)
    oth_weights = tuple(send(w, CORE) for w in own_weights)
    w_got = send(w_out, CORE)
    states, oth_weights, w_got, levels = fence(states, oth_weights, w_got, levels)

    sec = lax.axis_index("section")
    x, yh = sec // 2, sec % 2
    span = (sec + 7) % 8
    level = levels[span].reshape(1)

    def sid(dx, flip):
        return (((x + dx) % 4) * 2 + (yh ^ flip) + 7) % 8

    def ids(*which):
        return jnp.stack([span, *which])

    chip = jnp.concatenate([states, send(states, CORE)], axis=0)
    f1, g0 = send(chip, AWAY), send(states, ACROSS)
    w, mark = pack(own_weights + oth_weights)
    f1, g0, mark, w_got, level = fence(f1, g0, mark, w_got, level)

    f2, g1a = send(f1, AWAY), send(f1[:n], ACROSS)
    w_both = jnp.concatenate([w_out, w_got], axis=0)
    f2, g1a, w_both, f1 = fence(f2, g1a, w_both, f1)

    f3, g1b = send(f2, AWAY), send(f1[n:], ACROSS)
    f3, g1a, g1b, f1, f2 = fence(f3, g1a, g1b, f1, f2)
    g1 = jnp.concatenate([g1a, g1b], axis=0)

    g2, g3a = send(g1, AWAY), send(f3[:n], ACROSS)
    own1, oth1 = project(level, norm_gain, [states, f1, f2, f3, g0, g1], w)
    g2, g3a, f3, own1, oth1 = fence(g2, g3a, f3, own1, oth1)

    h, g3b = send(jnp.concatenate([f3[:n], g3a], axis=0), AWAY), send(f3[n:], ACROSS)
    oth1 = send(oth1, CORE)
    own2, oth2 = project(level, norm_gain, [g2, g3a], w)
    h, g3b, oth1, own2, oth2 = fence(h, g3b, oth1, own2, oth2)
    oth2 = send(oth2, CORE)
    own3, oth3 = project(level, norm_gain, [h, g3b], w)
    oth3 = send(oth3, CORE)
    q, kv = join((own1, own2, own3, oth1, oth2, oth3), ((0, 0, HD), (0, HD, 3 * HD)))

    a, b, p = fence(send_sec(kv, XUP), send_sec(kv, XDOWN), send_sec(kv, YH))
    c, pa, pb = send_sec(a, XUP), send_sec(a, YH), send_sec(p, XDOWN)
    near = ids(span, sid(-1, 0), sid(1, 0), sid(0, 1))
    state = attend(levels, near, q, [kv, a, b, p], None, False)
    c, pa, pb, state = fence(c, pa, pb, state)
    cut = kv.shape[0] // 2
    d = [send_sec(pa[:cut], XUP), send_sec(pb[cut:], XDOWN)]
    state = attend(levels, ids(sid(2, 0), sid(-1, 1), sid(1, 1)), q, [c, pa, pb], state, False)
    d, state = fence(d, state)
    att = attend(levels, ids(sid(2, 1), sid(2, 1)), q, d, state, True)

    count = att.shape[0] // 2
    partner = send(att[count:], CORE)
    ends = [sum(SETS[0]), sum(SETS[0]) + sum(SETS[1]), count]
    p3 = partials(att, partner, w_both, ends[1], SETS[2])
    p2 = partials(att, partner, w_both, ends[0], SETS[1])
    p1 = partials(att, partner, w_both, 0, SETS[0])
    m, f1, f2, f3, g0, g1 = p1
    g2, g3a = p2
    h, g3b = p3

    h, g3b = fence(send(h, HOME), send(g3b, ACROSS))
    g2, g3a = fence(send(g2, HOME), send(plus(g3a, h[n:]), ACROSS))
    g1 = plus(g1, g2)
    f3 = jnp.concatenate([plus(f3[:n], h[:n], g3a), plus(f3[n:], g3b)], axis=0)
    g1 = send(g1, ACROSS)
    f3, g0, m = fence(send(f3, HOME), g0, m)
    f2 = plus(f2, f3)
    f2, g1 = fence(send(f2, HOME), g1)
    f1, g0 = fence(send(plus(f1, f2, g1), HOME), send(g0, ACROSS))
    proj = m.astype(F32) + f1[:n].astype(F32) + g0.astype(F32) + send(f1[n:], CORE).astype(F32)
    gate = lax.dynamic_index_in_dim(out_gate, levels[span], 0, keepdims=True)
    return (states.astype(F32) + gate * proj).astype(BF16)


def solution(mesh):
    return jax.shard_map(
        shards,
        mesh=mesh,
        in_specs=(
            P(("section", "head"), None),
            P(),
            P("section", None),
            P(),
            P(),
            P(None, "head"),
            P(None, "head"),
            P(None, "head"),
            P("head", None),
        ),
        out_specs=P(("section", "head"), None),
        check_vma=False,
    )
```

```python
import functools
import math

import jax
import jax.numpy as jnp
from jax import lax
from jax.experimental import pallas as pl
from jax.experimental.pallas import tpu as pltpu
from jax.sharding import PartitionSpec as P

HD = 128
Z = 8
F32 = jnp.float32
BF16 = jnp.bfloat16
VMEM_LIMIT = 24 * 1024 * 1024
LOW = -3.0e38


def head_of(yl, z, core):
    return (yl * Z + z % Z) * 2 + core


def z_route(step):
    return [
        (head_of(yl, z, c), head_of(yl, z + step, c))
        for yl in range(2)
        for z in range(Z)
        for c in range(2)
    ]


AWAY = [r for r in z_route(1) if r[0] % 2 == 0] + [r for r in z_route(-1) if r[0] % 2 == 1]
HOME = [(j, i) for i, j in AWAY]
ACROSS = [(h, h ^ 16) for h in range(32)]
CORE = [(h, h ^ 1) for h in range(32)]


def x_route(step):
    return [(x * 2 + yh, ((x + step) % 4) * 2 + yh) for x in range(4) for yh in range(2)]


XUP, XDOWN = x_route(1), x_route(-1)
YH = [(s, s ^ 1) for s in range(8)]
NEXT = [(s, (s + 1) % 8) for s in range(8)]


def send(value, route):
    return lax.ppermute(value, "head", route)


def send_sec(value, route):
    return lax.ppermute(value, "section", route)


def fence(*values):
    return lax.optimization_barrier(values)


def params(**kw):
    return pltpu.CompilerParams(vmem_limit_bytes=VMEM_LIMIT, **kw)


def pack_kernel(*refs):
    for j, ref in enumerate(refs[:-1]):
        refs[-1][:, j * HD : (j + 1) * HD] = ref[...]


def pack(weights):
    d = weights[0].shape[0]
    n = len(weights)
    tile = d // 6
    return pl.pallas_call(
        pack_kernel,
        grid=(6,),
        in_specs=[pl.BlockSpec((tile, HD), lambda i: (i, 0))] * n,
        out_specs=pl.BlockSpec((tile, n * HD), lambda i: (i, 0)),
        out_shape=pltpu.VMEM((d, n * HD), BF16),
        compiler_params=params(),
        cost_estimate=pl.CostEstimate(flops=0, bytes_accessed=4 * n * d * HD, transcendentals=0),
        name="pack",
    )(*weights)


def project_kernel(n, d, level_ref, gain_ref, *refs):
    xs, (w_ref, own_ref, oth_ref, acc, ss) = refs[:n], refs[n:]
    k = pl.program_id(0)

    @pl.when(k == 0)
    def _():
        acc[...] = jnp.zeros_like(acc)
        ss[...] = jnp.zeros_like(ss)

    gain = gain_ref[pl.ds(level_ref[0], 1), :]
    x = jnp.concatenate([r[...] for r in xs], axis=0)
    part, scaled = None, []
    for i in range(x.shape[1] // HD):
        piece = x[:, i * HD : (i + 1) * HD].astype(F32)
        part = piece * piece if part is None else part + piece * piece
        scaled.append((piece * gain[:, i * HD : (i + 1) * HD]).astype(BF16))
    ss[...] += part
    acc[...] += jnp.dot(jnp.concatenate(scaled, axis=1), w_ref[...], preferred_element_type=F32)

    @pl.when(k == pl.num_programs(0) - 1)
    def _():
        r = lax.rsqrt(jnp.sum(ss[...], axis=1, keepdims=True) / d + 1e-06)
        rq = r * (math.log2(math.e) / math.sqrt(HD))
        for ref, base in ((own_ref, 0), (oth_ref, 3 * HD)):
            ref[:, :HD] = (acc[:, base : base + HD] * rq).astype(BF16)
            ref[:, HD:] = (acc[:, base + HD : base + 3 * HD] * r).astype(BF16)


def project(level, gain, blocks, w):
    d, cols = w.shape
    rows = sum(b.shape[0] for b in blocks)
    tile = 1024
    xspecs = [pl.BlockSpec((b.shape[0], tile), lambda k: (0, k)) for b in blocks]
    ospec = pl.BlockSpec((rows, cols // 2), lambda k: (0, 0))
    shape = jax.ShapeDtypeStruct((rows, cols // 2), BF16)
    return pl.pallas_call(
        functools.partial(project_kernel, len(blocks), d),
        grid=(d // tile,),
        in_specs=[
            pl.BlockSpec(memory_space=pltpu.SMEM),
            pl.BlockSpec((gain.shape[0], tile), lambda k: (0, k)),
            *xspecs,
            pl.BlockSpec((tile, cols), lambda k: (k, 0)),
        ],
        out_specs=[ospec, ospec],
        out_shape=[shape, shape],
        scratch_shapes=[pltpu.VMEM((rows, cols), F32), pltpu.VMEM((rows, HD), F32)],
        compiler_params=params(),
        cost_estimate=pl.CostEstimate(
            flops=2 * rows * d * cols, bytes_accessed=2 * d * (rows + cols), transcendentals=0
        ),
        name="project",
    )(level, gain, *blocks, w)


def join_kernel(columns, *refs):
    ins, outs = refs[: -len(columns)], refs[-len(columns) :]
    for ref, (first, lo, hi) in zip(outs, columns):
        at = 0
        for part in ins[first:]:
            rows = part.shape[0]
            ref[at : at + rows, :] = part[:, lo:hi]
            at += rows


def join(parts, columns):
    vm = pl.BlockSpec(memory_space=pltpu.VMEM)
    return pl.pallas_call(
        functools.partial(join_kernel, columns),
        in_specs=[vm] * len(parts),
        out_specs=[vm] * len(columns),
        out_shape=[
            jax.ShapeDtypeStruct((sum(p.shape[0] for p in parts[first:]), hi - lo), BF16)
            for first, lo, hi in columns
        ],
        compiler_params=params(),
        cost_estimate=pl.CostEstimate(flops=0, bytes_accessed=2000000, transcendentals=0),
        name="join",
    )(*parts)


def attend_kernel(n, first, levels_ref, ids_ref, *refs):
    q_ref, kvs, rest = refs[0], refs[1 : 1 + n], refs[1 + n :]
    m, acc = rest[-2:]
    if first:
        m[...] = jnp.full_like(m, LOW)
        acc[...] = jnp.zeros_like(acc)
    else:
        m[...] = rest[0][...]
        acc[...] = rest[1][...]
    mine = levels_ref[ids_ref[0]]
    for i in range(n):

        @pl.when(levels_ref[ids_ref[1 + i]] <= mine)
        def _(kv=kvs[i]):
            attend_block(q_ref, kv[...], m, acc, range(0, q_ref.shape[0], SUB), 0)


SUB = 128


def attend_block(q_ref, kv, m, acc, starts, base):
    k = kv[:, :HD]
    v = jnp.concatenate([kv[:, HD:], jnp.ones((kv.shape[0], HD), BF16)], axis=1)
    for at in starts:
        rows = slice(at, min(at + SUB, m.shape[0]))
        q = q_ref[base + rows.start : base + rows.stop, :]
        s = lax.dot_general(q, k, (((1,), (1,)), ((), ())), preferred_element_type=F32)
        old = m[rows, :]
        new = jnp.maximum(old, jnp.max(s, axis=1, keepdims=True))
        p = jnp.exp2(s - new[:, :1]).astype(BF16)
        added = jnp.dot(p, v, preferred_element_type=F32)
        scale = jnp.exp2(old - new)
        acc[rows, :] = acc[rows, :] * jnp.concatenate([scale, scale], axis=1) + added
        m[rows, :] = new


def attend(levels, ids, q, kvs, state):
    rows = q.shape[0]
    n = len(kvs)
    smem = pl.BlockSpec(memory_space=pltpu.SMEM)
    vm = pl.BlockSpec(memory_space=pltpu.VMEM)
    return pl.pallas_call(
        functools.partial(attend_kernel, n, state is None),
        in_specs=[smem, smem] + [vm] * (1 + n + (0 if state is None else 2)),
        out_specs=[vm, vm],
        out_shape=[
            jax.ShapeDtypeStruct((rows, HD), F32),
            jax.ShapeDtypeStruct((rows, 2 * HD), F32),
        ],
        compiler_params=params(),
        cost_estimate=pl.CostEstimate(
            flops=sum(8 * rows * kv.shape[0] * HD for kv in kvs),
            bytes_accessed=4 * rows * HD * 8,
            transcendentals=sum(rows * kv.shape[0] for kv in kvs),
        ),
        name="attend",
    )(levels, ids, q, *kvs, *(() if state is None else state))


def finish_kernel(n, lo, hi, levels_ref, ids_ref, q_ref, *refs):
    kvs, (m_in, acc_in, mine_ref, theirs_ref, m, acc) = refs[:n], refs[n:]
    m[...] = m_in[lo:hi, :]
    acc[...] = acc_in[lo:hi, :]

    @pl.when(levels_ref[ids_ref[1]] <= levels_ref[ids_ref[0]])
    def _():
        kv = jnp.concatenate([r[...] for r in kvs], axis=0)
        attend_block(q_ref, kv, m, acc, range(0, hi - lo, SUB), lo)

    out = (acc[:, :HD] / acc[:, HD:]).astype(BF16)
    half = (hi - lo) // 2
    mine_ref[...] = out[:half, :]
    theirs_ref[...] = out[half:, :]


def finish(levels, ids, q, kvs, state, lo, hi):
    n = len(kvs)
    rows = hi - lo
    smem = pl.BlockSpec(memory_space=pltpu.SMEM)
    vm = pl.BlockSpec(memory_space=pltpu.VMEM)
    return pl.pallas_call(
        functools.partial(finish_kernel, n, lo, hi),
        in_specs=[smem, smem] + [vm] * (3 + n),
        out_specs=[vm, vm],
        out_shape=[jax.ShapeDtypeStruct((rows // 2, HD), BF16)] * 2,
        scratch_shapes=[pltpu.VMEM((rows, HD), F32), pltpu.VMEM((rows, 2 * HD), F32)],
        compiler_params=params(),
        cost_estimate=pl.CostEstimate(
            flops=8 * rows * 1024 * HD, bytes_accessed=4 * rows * HD * 4, transcendentals=rows * 1024
        ),
        name="finish",
    )(levels, ids, q, *kvs, *state)


def partial_kernel(start, sizes, att_ref, partner_ref, w_ref, *outs):
    rows = slice(start, start + sum(sizes))
    a = jnp.concatenate([att_ref[rows, :], partner_ref[rows, :]], axis=1)
    step = 512
    for j in range(0, w_ref.shape[1], step):
        r = jnp.dot(a, w_ref[:, j : j + step], preferred_element_type=F32).astype(BF16)
        at = 0
        for size, ref in zip(sizes, outs):
            ref[:, j : j + step] = r[at : at + size]
            at += size


def partials(att, partner, w, start, sizes):
    rows, cols = sum(sizes), w.shape[1]
    vm = pl.BlockSpec(memory_space=pltpu.VMEM)
    return pl.pallas_call(
        functools.partial(partial_kernel, start, sizes),
        in_specs=[vm, vm, vm],
        out_specs=[vm] * len(sizes),
        out_shape=[jax.ShapeDtypeStruct((n, cols), BF16) for n in sizes],
        compiler_params=params(),
        cost_estimate=pl.CostEstimate(
            flops=4 * rows * HD * cols, bytes_accessed=2 * cols * (rows + 2 * HD), transcendentals=0
        ),
        name="partials",
    )(att, partner, w)


def plus(*terms):
    total = terms[0].astype(F32)
    for t in terms[1:]:
        total = total + t.astype(F32)
    return total.astype(BF16)


SETS = ((32, 64, 64, 64, 32, 64), (64, 32), (64, 32))


def shards(states, levels, span_mask, norm_gain, out_gate, w_query, w_key, w_value, w_out):
    n = states.shape[0]
    own_weights = (w_query, w_key, w_value)

    states = send_sec(states, NEXT)
    oth_weights = tuple(send(w, CORE) for w in own_weights)
    w_got = send(w_out, CORE)
    states, w_got, levels = fence(states, w_got, levels)

    sec = lax.axis_index("section")
    x, yh = sec // 2, sec % 2
    span = (sec + 7) % 8
    level = levels[span].reshape(1)

    def sid(dx, flip):
        return (((x + dx) % 4) * 2 + (yh ^ flip) + 7) % 8

    def ids(*which):
        return jnp.stack([span, *which])

    chip = jnp.concatenate([states, send(states, CORE)], axis=0)
    f1, g0 = send(chip, AWAY), send(states, ACROSS)
    w = pack(own_weights + oth_weights)
    f1, g0, w_got, level = fence(f1, g0, w_got, level)

    f2, g1a = send(f1, AWAY), send(f1[:n], ACROSS)
    w_both = jnp.concatenate([w_out, w_got], axis=0)
    f2, g1a, w_both, f1 = fence(f2, g1a, w_both, f1)

    f3, g1b = send(f2, AWAY), send(f1[n:], ACROSS)
    f3, g1a, g1b, f1, f2 = fence(f3, g1a, g1b, f1, f2)
    g1 = jnp.concatenate([g1a, g1b], axis=0)

    g2, g3a = send(g1, AWAY), send(f3[:n], ACROSS)
    own1, oth1 = project(level, norm_gain, [states, f1, f2, f3, g0, g1], w)
    g2, g3a, f3, own1, oth1 = fence(g2, g3a, f3, own1, oth1)

    h, g3b = send(jnp.concatenate([f3[:n], g3a], axis=0), AWAY), send(f3[n:], ACROSS)
    oth1 = send(oth1, CORE)
    own2, oth2 = project(level, norm_gain, [g2, g3a], w)
    h, g3b, oth1, own2, oth2 = fence(h, g3b, oth1, own2, oth2)
    oth2 = send(oth2, CORE)
    own3, oth3 = project(level, norm_gain, [h, g3b], w)
    oth3 = send(oth3, CORE)
    q, kv = join((own3, oth3, own1, own2, oth1, oth2), ((0, 0, HD), (0, HD, 3 * HD)))
    cut3 = 2 * own3.shape[0]

    p, a, b = fence(send_sec(kv, YH), send_sec(kv, XUP), send_sec(kv, XDOWN))
    pa, c, pb = send_sec(a, YH), send_sec(a, XUP), send_sec(p, XDOWN)
    near = ids(span, sid(-1, 0), sid(1, 0), sid(0, 1))
    state = attend(levels, near, q, [kv, a, b, p], None)
    c, pa, pb, state = fence(c, pa, pb, state)
    cut = kv.shape[0] // 2
    d = [send_sec(pa[:cut], XUP), send_sec(pb[cut:], XDOWN)]
    state = attend(levels, ids(sid(2, 0), sid(-1, 1), sid(1, 1)), q, [c, pa, pb], state)
    d, state = fence(d, state)
    far = ids(sid(2, 1))
    mine, theirs = finish(levels, far, q, d, state, 0, cut3)

    p3 = partials(mine, send(theirs, CORE), w_both, 0, SETS[2])
    mine, theirs = finish(levels, far, q, d, state, cut3, q.shape[0])
    theirs = send(theirs, CORE)
    p2 = partials(mine, theirs, w_both, sum(SETS[0]), SETS[1])
    p1 = partials(mine, theirs, w_both, 0, SETS[0])
    m, f1, f2, f3, g0, g1 = p1
    g2, g3a = p2
    h, g3b = p3

    h, g3b = fence(send(h, HOME), send(g3b, ACROSS))
    g2, g3a = fence(send(g2, HOME), send(plus(g3a, h[n:]), ACROSS))
    g1 = plus(g1, g2)
    f3 = jnp.concatenate([plus(f3[:n], h[:n], g3a), plus(f3[n:], g3b)], axis=0)
    g1 = send(g1, ACROSS)
    f3, g0, m = fence(send(f3, HOME), g0, m)
    f2 = plus(f2, f3)
    f2, g1 = fence(send(f2, HOME), g1)
    f1, g0 = fence(send(plus(f1, f2, g1), HOME), send(g0, ACROSS))
    proj = m.astype(F32) + f1[:n].astype(F32) + g0.astype(F32) + send(f1[n:], CORE).astype(F32)
    gate = lax.dynamic_index_in_dim(out_gate, levels[span], 0, keepdims=True)
    return (states.astype(F32) + gate * proj).astype(BF16)


def solution(mesh):
    return jax.shard_map(
        shards,
        mesh=mesh,
        in_specs=(
            P(("section", "head"), None),
            P(),
            P("section", None),
            P(),
            P(),
            P(None, "head"),
            P(None, "head"),
            P(None, "head"),
            P("head", None),
        ),
        out_specs=P(("section", "head"), None),
        check_vma=False,
    )
```

```python
import functools
import math

import jax
import jax.numpy as jnp
from jax import lax
from jax.experimental import pallas as pl
from jax.experimental.pallas import tpu as pltpu
from jax.sharding import PartitionSpec as P

HD = 128
Z = 8
F32 = jnp.float32
BF16 = jnp.bfloat16
VMEM_LIMIT = 24 * 1024 * 1024
LOW = -3.0e38


def head_of(yl, z, core):
    return (yl * Z + z % Z) * 2 + core


def z_route(step):
    return [
        (head_of(yl, z, c), head_of(yl, z + step, c))
        for yl in range(2)
        for z in range(Z)
        for c in range(2)
    ]


AWAY = [r for r in z_route(1) if r[0] % 2 == 0] + [r for r in z_route(-1) if r[0] % 2 == 1]
HOME = [(j, i) for i, j in AWAY]
ACROSS = [(h, h ^ 16) for h in range(32)]
OVER = [(h, h ^ 17) for h in range(32)]
CORE = [(h, h ^ 1) for h in range(32)]


def x_route(step):
    return [(x * 2 + yh, ((x + step) % 4) * 2 + yh) for x in range(4) for yh in range(2)]


XUP, XDOWN = x_route(1), x_route(-1)
YH = [(s, s ^ 1) for s in range(8)]
NEXT = [(s, (s + 1) % 8) for s in range(8)]


def send(value, route):
    return lax.ppermute(value, "head", route)


def send_sec(value, route):
    return lax.ppermute(value, "section", route)


def fence(*values):
    return lax.optimization_barrier(values)


def params(**kw):
    return pltpu.CompilerParams(vmem_limit_bytes=VMEM_LIMIT, **kw)


def pack_kernel(*refs):
    for j, ref in enumerate(refs[:-1]):
        refs[-1][:, j * HD : (j + 1) * HD] = ref[...]


def pack(weights):
    d = weights[0].shape[0]
    n = len(weights)
    tile = d // 6
    return pl.pallas_call(
        pack_kernel,
        grid=(6,),
        in_specs=[pl.BlockSpec((tile, HD), lambda i: (i, 0))] * n,
        out_specs=pl.BlockSpec((tile, n * HD), lambda i: (i, 0)),
        out_shape=pltpu.VMEM((d, n * HD), BF16),
        compiler_params=params(),
        cost_estimate=pl.CostEstimate(flops=0, bytes_accessed=4 * n * d * HD, transcendentals=0),
        name="pack",
    )(*weights)


def project_kernel(n, d, level_ref, gain_ref, *refs):
    xs, (w_ref, own_ref, oth_ref, acc, ss) = refs[:n], refs[n:]
    k = pl.program_id(0)

    @pl.when(k == 0)
    def _():
        acc[...] = jnp.zeros_like(acc)
        ss[...] = jnp.zeros_like(ss)

    gain = gain_ref[pl.ds(level_ref[0], 1), :]
    x = jnp.concatenate([r[...] for r in xs], axis=0)
    part, scaled = None, []
    for i in range(x.shape[1] // HD):
        piece = x[:, i * HD : (i + 1) * HD].astype(F32)
        part = piece * piece if part is None else part + piece * piece
        scaled.append((piece * gain[:, i * HD : (i + 1) * HD]).astype(BF16))
    ss[...] += part
    acc[...] += jnp.dot(jnp.concatenate(scaled, axis=1), w_ref[...], preferred_element_type=F32)

    @pl.when(k == pl.num_programs(0) - 1)
    def _():
        r = lax.rsqrt(jnp.sum(ss[...], axis=1, keepdims=True) / d + 1e-06)
        rq = r * (math.log2(math.e) / math.sqrt(HD))
        for ref, base in ((own_ref, 0), (oth_ref, 3 * HD)):
            ref[:, :HD] = (acc[:, base : base + HD] * rq).astype(BF16)
            ref[:, HD:] = (acc[:, base + HD : base + 3 * HD] * r).astype(BF16)


def project(level, gain, blocks, w):
    d, cols = w.shape
    rows = sum(b.shape[0] for b in blocks)
    tile = 1024
    xspecs = [pl.BlockSpec((b.shape[0], tile), lambda k: (0, k)) for b in blocks]
    ospec = pl.BlockSpec((rows, cols // 2), lambda k: (0, 0))
    shape = jax.ShapeDtypeStruct((rows, cols // 2), BF16)
    return pl.pallas_call(
        functools.partial(project_kernel, len(blocks), d),
        grid=(d // tile,),
        in_specs=[
            pl.BlockSpec(memory_space=pltpu.SMEM),
            pl.BlockSpec((gain.shape[0], tile), lambda k: (0, k)),
            *xspecs,
            pl.BlockSpec((tile, cols), lambda k: (k, 0)),
        ],
        out_specs=[ospec, ospec],
        out_shape=[shape, shape],
        scratch_shapes=[pltpu.VMEM((rows, cols), F32), pltpu.VMEM((rows, HD), F32)],
        compiler_params=params(),
        cost_estimate=pl.CostEstimate(
            flops=2 * rows * d * cols, bytes_accessed=2 * d * (rows + cols), transcendentals=0
        ),
        name="project",
    )(level, gain, *blocks, w)


def join_kernel(columns, *refs):
    ins, outs = refs[: -len(columns)], refs[-len(columns) :]
    for ref, (first, lo, hi) in zip(outs, columns):
        at = 0
        for part in ins[first:]:
            rows = part.shape[0]
            ref[at : at + rows, :] = part[:, lo:hi]
            at += rows


def join(parts, columns):
    vm = pl.BlockSpec(memory_space=pltpu.VMEM)
    return pl.pallas_call(
        functools.partial(join_kernel, columns),
        in_specs=[vm] * len(parts),
        out_specs=[vm] * len(columns),
        out_shape=[
            jax.ShapeDtypeStruct((sum(p.shape[0] for p in parts[first:]), hi - lo), BF16)
            for first, lo, hi in columns
        ],
        compiler_params=params(),
        cost_estimate=pl.CostEstimate(flops=0, bytes_accessed=2000000, transcendentals=0),
        name="join",
    )(*parts)


def attend_kernel(n, first, levels_ref, ids_ref, *refs):
    q_ref, kvs, rest = refs[0], refs[1 : 1 + n], refs[1 + n :]
    m, acc = rest[-2:]
    if first:
        m[...] = jnp.full_like(m, LOW)
        acc[...] = jnp.zeros_like(acc)
    else:
        m[...] = rest[0][...]
        acc[...] = rest[1][...]
    mine = levels_ref[ids_ref[0]]
    for i in range(n):

        @pl.when(levels_ref[ids_ref[1 + i]] <= mine)
        def _(kv=kvs[i]):
            attend_block(q_ref, kv[...], m, acc, range(0, q_ref.shape[0], SUB), 0)


SUB = 128


def attend_block(q_ref, kv, m, acc, starts, base):
    k = kv[:, :HD]
    v = jnp.concatenate([kv[:, HD:], jnp.ones((kv.shape[0], HD), BF16)], axis=1)
    for at in starts:
        rows = slice(at, min(at + SUB, m.shape[0]))
        q = q_ref[base + rows.start : base + rows.stop, :]
        s = lax.dot_general(q, k, (((1,), (1,)), ((), ())), preferred_element_type=F32)
        old = m[rows, :]
        new = jnp.maximum(old, jnp.max(s, axis=1, keepdims=True))
        p = jnp.exp2(s - new[:, :1]).astype(BF16)
        added = jnp.dot(p, v, preferred_element_type=F32)
        scale = jnp.exp2(old - new)
        acc[rows, :] = acc[rows, :] * jnp.concatenate([scale, scale], axis=1) + added
        m[rows, :] = new


def attend(levels, ids, q, kvs, state):
    rows = q.shape[0]
    n = len(kvs)
    smem = pl.BlockSpec(memory_space=pltpu.SMEM)
    vm = pl.BlockSpec(memory_space=pltpu.VMEM)
    return pl.pallas_call(
        functools.partial(attend_kernel, n, state is None),
        in_specs=[smem, smem] + [vm] * (1 + n + (0 if state is None else 2)),
        out_specs=[vm, vm],
        out_shape=[
            jax.ShapeDtypeStruct((rows, HD), F32),
            jax.ShapeDtypeStruct((rows, 2 * HD), F32),
        ],
        compiler_params=params(),
        cost_estimate=pl.CostEstimate(
            flops=sum(8 * rows * kv.shape[0] * HD for kv in kvs),
            bytes_accessed=4 * rows * HD * 8,
            transcendentals=sum(rows * kv.shape[0] for kv in kvs),
        ),
        name="attend",
    )(levels, ids, q, *kvs, *(() if state is None else state))


def finish_kernel(n, lo, hi, levels_ref, ids_ref, q_ref, *refs):
    kvs, (m_in, acc_in, mine_ref, theirs_ref, m, acc) = refs[:n], refs[n:]
    m[...] = m_in[lo:hi, :]
    acc[...] = acc_in[lo:hi, :]

    @pl.when(levels_ref[ids_ref[1]] <= levels_ref[ids_ref[0]])
    def _():
        kv = jnp.concatenate([r[...] for r in kvs], axis=0)
        attend_block(q_ref, kv, m, acc, range(0, hi - lo, SUB), lo)

    out = (acc[:, :HD] / acc[:, HD:]).astype(BF16)
    half = (hi - lo) // 2
    mine_ref[...] = out[:half, :]
    theirs_ref[...] = out[half:, :]


def finish(levels, ids, q, kvs, state, lo, hi):
    n = len(kvs)
    rows = hi - lo
    smem = pl.BlockSpec(memory_space=pltpu.SMEM)
    vm = pl.BlockSpec(memory_space=pltpu.VMEM)
    return pl.pallas_call(
        functools.partial(finish_kernel, n, lo, hi),
        in_specs=[smem, smem] + [vm] * (3 + n),
        out_specs=[vm, vm],
        out_shape=[jax.ShapeDtypeStruct((rows // 2, HD), BF16)] * 2,
        scratch_shapes=[pltpu.VMEM((rows, HD), F32), pltpu.VMEM((rows, 2 * HD), F32)],
        compiler_params=params(),
        cost_estimate=pl.CostEstimate(
            flops=8 * rows * 1024 * HD, bytes_accessed=4 * rows * HD * 4, transcendentals=rows * 1024
        ),
        name="finish",
    )(levels, ids, q, *kvs, *state)


def partial_kernel(start, sizes, att_ref, partner_ref, w_ref, *outs):
    rows = slice(start, start + sum(sizes))
    a = jnp.concatenate([att_ref[rows, :], partner_ref[rows, :]], axis=1)
    step = 512
    for j in range(0, w_ref.shape[1], step):
        r = jnp.dot(a, w_ref[:, j : j + step], preferred_element_type=F32).astype(BF16)
        at = 0
        for size, ref in zip(sizes, outs):
            ref[:, j : j + step] = r[at : at + size]
            at += size


def partials(att, partner, w, start, sizes):
    rows, cols = sum(sizes), w.shape[1]
    vm = pl.BlockSpec(memory_space=pltpu.VMEM)
    return pl.pallas_call(
        functools.partial(partial_kernel, start, sizes),
        in_specs=[vm, vm, vm],
        out_specs=[vm] * len(sizes),
        out_shape=[jax.ShapeDtypeStruct((n, cols), BF16) for n in sizes],
        compiler_params=params(),
        cost_estimate=pl.CostEstimate(
            flops=4 * rows * HD * cols, bytes_accessed=2 * cols * (rows + 2 * HD), transcendentals=0
        ),
        name="partials",
    )(att, partner, w)


def plus(*terms):
    total = terms[0].astype(F32)
    for t in terms[1:]:
        total = total + t.astype(F32)
    return total.astype(BF16)


SETS = ((32, 64, 64, 64, 32, 64), (64, 32, 32), (32, 32))


def shards(states, levels, span_mask, norm_gain, out_gate, w_query, w_key, w_value, w_out):
    n = states.shape[0]
    own_weights = (w_query, w_key, w_value)

    states = send_sec(states, NEXT)
    oth_weights = tuple(send(w, CORE) for w in own_weights)
    w_got = send(w_out, CORE)
    states, w_got, levels = fence(states, w_got, levels)

    sec = lax.axis_index("section")
    x, yh = sec // 2, sec % 2
    span = (sec + 7) % 8
    level = levels[span].reshape(1)

    def sid(dx, flip):
        return (((x + dx) % 4) * 2 + (yh ^ flip) + 7) % 8

    def ids(*which):
        return jnp.stack([span, *which])

    chip = jnp.concatenate([states, send(states, CORE)], axis=0)
    f1, g0 = send(chip, AWAY), send(states, ACROSS)
    w = pack(own_weights + oth_weights)
    f1, g0, w_got, level = fence(f1, g0, w_got, level)

    f2, g1a = send(f1, AWAY), send(f1[:n], OVER)
    w_both = jnp.concatenate([w_out, w_got], axis=0)
    f2, g1a, w_both, f1 = fence(f2, g1a, w_both, f1)

    f3, g2a, g1b = send(f2, AWAY), send(g1a, HOME), send(f1[n:], OVER)
    f3, g2a, g1a, g1b, f1, f2 = fence(f3, g2a, g1a, g1b, f1, f2)

    g2b, g3a, f4 = send(g1b, HOME), send(f3[:n], OVER), send(f3[:n], AWAY)
    own1, oth1 = project(level, norm_gain, [states, f1, f2, f3, g0, g1a, g1b], w)
    g2b, g3a, f4, f3, own1, oth1 = fence(g2b, g3a, f4, f3, own1, oth1)

    g4, g3b = send(g3a, HOME), send(f3[n:], OVER)
    oth1 = send(oth1, CORE)
    own2, oth2 = project(level, norm_gain, [g2a, g2b, g3a, f4], w)
    g4, g3b, oth1, own2, oth2 = fence(g4, g3b, oth1, own2, oth2)
    oth2 = send(oth2, CORE)
    own3, oth3 = project(level, norm_gain, [g4, g3b], w)
    oth3 = send(oth3, CORE)
    q, kv = join((own3, oth3, own1, own2, oth1, oth2), ((0, 0, HD), (0, HD, 3 * HD)))
    cut3 = 2 * own3.shape[0]

    p, a, b = fence(send_sec(kv, YH), send_sec(kv, XUP), send_sec(kv, XDOWN))
    pa, c, pb = send_sec(a, YH), send_sec(a, XUP), send_sec(p, XDOWN)
    near = ids(span, sid(-1, 0), sid(1, 0), sid(0, 1))
    state = attend(levels, near, q, [kv, a, b, p], None)
    c, pa, pb, state = fence(c, pa, pb, state)
    cut = kv.shape[0] // 2
    d = [send_sec(pa[:cut], XUP), send_sec(pb[cut:], XDOWN)]
    state = attend(levels, ids(sid(2, 0), sid(-1, 1), sid(1, 1)), q, [c, pa, pb], state)
    d, state = fence(d, state)
    far = ids(sid(2, 1))
    mine, theirs = finish(levels, far, q, d, state, 0, cut3)

    p3 = partials(mine, send(theirs, CORE), w_both, 0, SETS[2])
    mine, theirs = finish(levels, far, q, d, state, cut3, q.shape[0])
    theirs = send(theirs, CORE)
    p2 = partials(mine, theirs, w_both, sum(SETS[0]), SETS[1])
    p1 = partials(mine, theirs, w_both, 0, SETS[0])
    m, f1, f2, f3, g0, g1 = p1
    g2, g3a, f4 = p2
    g4, g3b = p3

    g4, g3b = fence(send(g4, AWAY), send(g3b, OVER))
    g2, f4, g3a = fence(send(g2, AWAY), send(f4, HOME), send(plus(g3a, g4), OVER))
    g1 = plus(g1, g2)
    f3 = jnp.concatenate([plus(f3[:n], f4, g3a), plus(f3[n:], g3b)], axis=0)
    g1 = send(g1, OVER)
    f3, g0, m = fence(send(f3, HOME), g0, m)
    f2 = plus(f2, f3)
    f2, g1 = fence(send(f2, HOME), g1)
    f1, g0 = fence(send(plus(f1, f2, g1), HOME), send(g0, ACROSS))
    proj = m.astype(F32) + f1[:n].astype(F32) + g0.astype(F32) + send(f1[n:], CORE).astype(F32)
    gate = lax.dynamic_index_in_dim(out_gate, levels[span], 0, keepdims=True)
    return (states.astype(F32) + gate * proj).astype(BF16)


def solution(mesh):
    return jax.shard_map(
        shards,
        mesh=mesh,
        in_specs=(
            P(("section", "head"), None),
            P(),
            P("section", None),
            P(),
            P(),
            P(None, "head"),
            P(None, "head"),
            P(None, "head"),
            P("head", None),
        ),
        out_specs=P(("section", "head"), None),
        check_vma=False,
    )
```

```python
import functools
import math

import jax
import jax.numpy as jnp
from jax import lax
from jax.experimental import pallas as pl
from jax.experimental.pallas import tpu as pltpu
from jax.sharding import PartitionSpec as P

HD = 128
Z = 8
F32 = jnp.float32
BF16 = jnp.bfloat16
VMEM_LIMIT = 24 * 1024 * 1024
LOW = -3.0e38


def head_of(yl, z, core):
    return (yl * Z + z % Z) * 2 + core


def z_route(step):
    return [
        (head_of(yl, z, c), head_of(yl, z + step, c))
        for yl in range(2)
        for z in range(Z)
        for c in range(2)
    ]


AWAY = [r for r in z_route(1) if r[0] % 2 == 0] + [r for r in z_route(-1) if r[0] % 2 == 1]
HOME = [(j, i) for i, j in AWAY]
ACROSS = [(h, h ^ 16) for h in range(32)]
OVER = [(h, h ^ 17) for h in range(32)]
CORE = [(h, h ^ 1) for h in range(32)]


def x_route(step):
    return [(x * 2 + yh, ((x + step) % 4) * 2 + yh) for x in range(4) for yh in range(2)]


XUP, XDOWN = x_route(1), x_route(-1)
YH = [(s, s ^ 1) for s in range(8)]
NEXT = [(s, (s + 1) % 8) for s in range(8)]


def send(value, route):
    return lax.ppermute(value, "head", route)


def send_sec(value, route):
    return lax.ppermute(value, "section", route)


def fence(*values):
    return lax.optimization_barrier(values)


def params(**kw):
    return pltpu.CompilerParams(vmem_limit_bytes=VMEM_LIMIT, **kw)


def pack_kernel(*refs):
    for j, ref in enumerate(refs[:-1]):
        refs[-1][:, j * HD : (j + 1) * HD] = ref[...]


def pack(weights):
    d = weights[0].shape[0]
    n = len(weights)
    tile = d // 6
    return pl.pallas_call(
        pack_kernel,
        grid=(6,),
        in_specs=[pl.BlockSpec((tile, HD), lambda i: (i, 0))] * n,
        out_specs=pl.BlockSpec((tile, n * HD), lambda i: (i, 0)),
        out_shape=pltpu.VMEM((d, n * HD), BF16),
        compiler_params=params(),
        cost_estimate=pl.CostEstimate(flops=0, bytes_accessed=4 * n * d * HD, transcendentals=0),
        name="pack",
    )(*weights)


def project_kernel(n, d, level_ref, gain_ref, *refs):
    xs, (w_ref, own_ref, oth_ref, acc, ss) = refs[:n], refs[n:]
    k = pl.program_id(0)

    @pl.when(k == 0)
    def _():
        acc[...] = jnp.zeros_like(acc)
        ss[...] = jnp.zeros_like(ss)

    gain = gain_ref[pl.ds(level_ref[0], 1), :]
    x = jnp.concatenate([r[...] for r in xs], axis=0)
    part, scaled = None, []
    for i in range(x.shape[1] // HD):
        piece = x[:, i * HD : (i + 1) * HD].astype(F32)
        part = piece * piece if part is None else part + piece * piece
        scaled.append((piece * gain[:, i * HD : (i + 1) * HD]).astype(BF16))
    ss[...] += part
    acc[...] += jnp.dot(jnp.concatenate(scaled, axis=1), w_ref[...], preferred_element_type=F32)

    @pl.when(k == pl.num_programs(0) - 1)
    def _():
        r = lax.rsqrt(jnp.sum(ss[...], axis=1, keepdims=True) / d + 1e-06)
        rq = r * (math.log2(math.e) / math.sqrt(HD))
        for ref, base in ((own_ref, 0), (oth_ref, 3 * HD)):
            ref[:, :HD] = (acc[:, base : base + HD] * rq).astype(BF16)
            ref[:, HD:] = (acc[:, base + HD : base + 3 * HD] * r).astype(BF16)


def project(level, gain, blocks, w):
    d, cols = w.shape
    rows = sum(b.shape[0] for b in blocks)
    tile = 1024
    xspecs = [pl.BlockSpec((b.shape[0], tile), lambda k: (0, k)) for b in blocks]
    ospec = pl.BlockSpec((rows, cols // 2), lambda k: (0, 0))
    shape = jax.ShapeDtypeStruct((rows, cols // 2), BF16)
    return pl.pallas_call(
        functools.partial(project_kernel, len(blocks), d),
        grid=(d // tile,),
        in_specs=[
            pl.BlockSpec(memory_space=pltpu.SMEM),
            pl.BlockSpec((gain.shape[0], tile), lambda k: (0, k)),
            *xspecs,
            pl.BlockSpec((tile, cols), lambda k: (k, 0)),
        ],
        out_specs=[ospec, ospec],
        out_shape=[shape, shape],
        scratch_shapes=[pltpu.VMEM((rows, cols), F32), pltpu.VMEM((rows, HD), F32)],
        compiler_params=params(),
        cost_estimate=pl.CostEstimate(
            flops=2 * rows * d * cols, bytes_accessed=2 * d * (rows + cols), transcendentals=0
        ),
        name="project",
    )(level, gain, *blocks, w)


def join_kernel(columns, *refs):
    ins, outs = refs[: -len(columns)], refs[-len(columns) :]
    for ref, (first, lo, hi) in zip(outs, columns):
        at = 0
        for part in ins[first:]:
            rows = part.shape[0]
            ref[at : at + rows, :] = part[:, lo:hi]
            at += rows


def join(parts, columns):
    vm = pl.BlockSpec(memory_space=pltpu.VMEM)
    return pl.pallas_call(
        functools.partial(join_kernel, columns),
        in_specs=[vm] * len(parts),
        out_specs=[vm] * len(columns),
        out_shape=[
            jax.ShapeDtypeStruct((sum(p.shape[0] for p in parts[first:]), hi - lo), BF16)
            for first, lo, hi in columns
        ],
        compiler_params=params(),
        cost_estimate=pl.CostEstimate(flops=0, bytes_accessed=2000000, transcendentals=0),
        name="join",
    )(*parts)


def attend_kernel(n, first, levels_ref, ids_ref, *refs):
    q_ref, kvs, rest = refs[0], refs[1 : 1 + n], refs[1 + n :]
    m, acc = rest[-2:]
    if first:
        m[...] = jnp.full_like(m, LOW)
        acc[...] = jnp.zeros_like(acc)
    else:
        m[...] = rest[0][...]
        acc[...] = rest[1][...]
    mine = levels_ref[ids_ref[0]]
    for i in range(n):

        @pl.when(levels_ref[ids_ref[1 + i]] <= mine)
        def _(kv=kvs[i]):
            attend_block(q_ref, kv[...], m, acc, range(0, q_ref.shape[0], SUB), 0)


SUB = 128


def attend_block(q_ref, kv, m, acc, starts, base):
    k = kv[:, :HD]
    v = jnp.concatenate([kv[:, HD:], jnp.ones((kv.shape[0], HD), BF16)], axis=1)
    for at in starts:
        rows = slice(at, min(at + SUB, m.shape[0]))
        q = q_ref[base + rows.start : base + rows.stop, :]
        s = lax.dot_general(q, k, (((1,), (1,)), ((), ())), preferred_element_type=F32)
        old = m[rows, :]
        new = jnp.maximum(old, jnp.max(s, axis=1, keepdims=True))
        p = jnp.exp2(s - new[:, :1]).astype(BF16)
        added = jnp.dot(p, v, preferred_element_type=F32)
        scale = jnp.exp2(old - new)
        acc[rows, :] = acc[rows, :] * jnp.concatenate([scale, scale], axis=1) + added
        m[rows, :] = new


def attend(levels, ids, q, kvs, state):
    rows = q.shape[0]
    n = len(kvs)
    smem = pl.BlockSpec(memory_space=pltpu.SMEM)
    vm = pl.BlockSpec(memory_space=pltpu.VMEM)
    return pl.pallas_call(
        functools.partial(attend_kernel, n, state is None),
        in_specs=[smem, smem] + [vm] * (1 + n + (0 if state is None else 2)),
        out_specs=[vm, vm],
        out_shape=[
            jax.ShapeDtypeStruct((rows, HD), F32),
            jax.ShapeDtypeStruct((rows, 2 * HD), F32),
        ],
        compiler_params=params(),
        cost_estimate=pl.CostEstimate(
            flops=sum(8 * rows * kv.shape[0] * HD for kv in kvs),
            bytes_accessed=4 * rows * HD * 8,
            transcendentals=sum(rows * kv.shape[0] for kv in kvs),
        ),
        name="attend",
    )(levels, ids, q, *kvs, *(() if state is None else state))


def finish_kernel(n, lo, hi, levels_ref, ids_ref, q_ref, *refs):
    kvs, (m_in, acc_in, mine_ref, theirs_ref, m, acc) = refs[:n], refs[n:]
    m[...] = m_in[lo:hi, :]
    acc[...] = acc_in[lo:hi, :]

    @pl.when(levels_ref[ids_ref[1]] <= levels_ref[ids_ref[0]])
    def _():
        kv = jnp.concatenate([r[...] for r in kvs], axis=0)
        attend_block(q_ref, kv, m, acc, range(0, hi - lo, SUB), lo)

    out = (acc[:, :HD] / acc[:, HD:]).astype(BF16)
    half = (hi - lo) // 2
    mine_ref[...] = out[:half, :]
    theirs_ref[...] = out[half:, :]


def finish(levels, ids, q, kvs, state, lo, hi):
    n = len(kvs)
    rows = hi - lo
    smem = pl.BlockSpec(memory_space=pltpu.SMEM)
    vm = pl.BlockSpec(memory_space=pltpu.VMEM)
    return pl.pallas_call(
        functools.partial(finish_kernel, n, lo, hi),
        in_specs=[smem, smem] + [vm] * (3 + n),
        out_specs=[vm, vm],
        out_shape=[jax.ShapeDtypeStruct((rows // 2, HD), BF16)] * 2,
        scratch_shapes=[pltpu.VMEM((rows, HD), F32), pltpu.VMEM((rows, 2 * HD), F32)],
        compiler_params=params(),
        cost_estimate=pl.CostEstimate(
            flops=8 * rows * 1024 * HD, bytes_accessed=4 * rows * HD * 4, transcendentals=rows * 1024
        ),
        name="finish",
    )(levels, ids, q, *kvs, *state)


def partial_kernel(start, sizes, att_ref, partner_ref, w_ref, *outs):
    rows = slice(start, start + sum(sizes))
    a = jnp.concatenate([att_ref[rows, :], partner_ref[rows, :]], axis=1)
    step = 512
    for j in range(0, w_ref.shape[1], step):
        r = jnp.dot(a, w_ref[:, j : j + step], preferred_element_type=F32).astype(BF16)
        at = 0
        for size, ref in zip(sizes, outs):
            ref[:, j : j + step] = r[at : at + size]
            at += size


def partials(att, partner, w, start, sizes):
    rows, cols = sum(sizes), w.shape[1]
    vm = pl.BlockSpec(memory_space=pltpu.VMEM)
    return pl.pallas_call(
        functools.partial(partial_kernel, start, sizes),
        in_specs=[vm, vm, vm],
        out_specs=[vm] * len(sizes),
        out_shape=[jax.ShapeDtypeStruct((n, cols), BF16) for n in sizes],
        compiler_params=params(),
        cost_estimate=pl.CostEstimate(
            flops=4 * rows * HD * cols, bytes_accessed=2 * cols * (rows + 2 * HD), transcendentals=0
        ),
        name="partials",
    )(att, partner, w)


def plus(*terms):
    total = terms[0].astype(F32)
    for t in terms[1:]:
        total = total + t.astype(F32)
    return total.astype(BF16)


SETS = ((32, 64, 64, 64, 32, 64), (64, 32), (32, 32, 32))


def shards(states, levels, span_mask, norm_gain, out_gate, w_query, w_key, w_value, w_out):
    n = states.shape[0]
    own_weights = (w_query, w_key, w_value)

    states = send_sec(states, NEXT)
    oth_weights = tuple(send(w, CORE) for w in own_weights)
    w_got = send(w_out, CORE)
    states, w_got, levels = fence(states, w_got, levels)

    sec = lax.axis_index("section")
    x, yh = sec // 2, sec % 2
    span = (sec + 7) % 8
    level = levels[span].reshape(1)

    def sid(dx, flip):
        return (((x + dx) % 4) * 2 + (yh ^ flip) + 7) % 8

    def ids(*which):
        return jnp.stack([span, *which])

    chip = jnp.concatenate([states, send(states, CORE)], axis=0)
    f1, g0 = send(chip, AWAY), send(states, ACROSS)
    w = pack(own_weights + oth_weights)
    f1, g0, w_got, level = fence(f1, g0, w_got, level)

    f2, g1a = send(f1, AWAY), send(f1[:n], OVER)
    w_both = jnp.concatenate([w_out, w_got], axis=0)
    f2, g1a, w_both, f1 = fence(f2, g1a, w_both, f1)

    f3, g1b = send(f2, AWAY), send(f1[n:], OVER)
    f3, g1a, g1b, f1, f2 = fence(f3, g1a, g1b, f1, f2)
    g1 = jnp.concatenate([g1a, g1b], axis=0)

    g2, g3a = send(g1, HOME), send(f3[:n], OVER)
    own1, oth1 = project(level, norm_gain, [states, f1, f2, f3, g0, g1], w)
    g2, g3a, f3, own1, oth1 = fence(g2, g3a, f3, own1, oth1)

    g4, f4, g3b = send(g3a, HOME), send(f3[:n], AWAY), send(f3[n:], OVER)
    oth1 = send(oth1, CORE)
    own2, oth2 = project(level, norm_gain, [g2, g3a], w)
    g4, f4, g3b, oth1, own2, oth2 = fence(g4, f4, g3b, oth1, own2, oth2)
    oth2 = send(oth2, CORE)
    own3, oth3 = project(level, norm_gain, [f4, g4, g3b], w)
    oth3 = send(oth3, CORE)
    q, kv = join((own3, oth3, own1, own2, oth1, oth2), ((0, 0, HD), (0, HD, 3 * HD)))
    cut3 = 2 * own3.shape[0]

    p, a, b = fence(send_sec(kv, YH), send_sec(kv, XUP), send_sec(kv, XDOWN))
    pa, c, pb = send_sec(a, YH), send_sec(a, XUP), send_sec(p, XDOWN)
    near = ids(span, sid(-1, 0), sid(1, 0), sid(0, 1))
    state = attend(levels, near, q, [kv, a, b, p], None)
    c, pa, pb, state = fence(c, pa, pb, state)
    cut = kv.shape[0] // 2
    d = [send_sec(pa[:cut], XUP), send_sec(pb[cut:], XDOWN)]
    state = attend(levels, ids(sid(2, 0), sid(-1, 1), sid(1, 1)), q, [c, pa, pb], state)
    d, state = fence(d, state)
    far = ids(sid(2, 1))
    mine, theirs = finish(levels, far, q, d, state, 0, cut3)

    p3 = partials(mine, send(theirs, CORE), w_both, 0, SETS[2])
    mine, theirs = finish(levels, far, q, d, state, cut3, q.shape[0])
    theirs = send(theirs, CORE)
    p2 = partials(mine, theirs, w_both, sum(SETS[0]), SETS[1])
    p1 = partials(mine, theirs, w_both, 0, SETS[0])
    m, f1, f2, f3, g0, g1 = p1
    g2, g3a = p2
    f4, g4, g3b = p3

    g4, f4, g3b = fence(send(g4, AWAY), send(f4, HOME), send(g3b, OVER))
    g2, g3a = fence(send(g2, AWAY), send(plus(g3a, g4), OVER))
    g1 = plus(g1, g2)
    f3 = jnp.concatenate([plus(f3[:n], f4, g3a), plus(f3[n:], g3b)], axis=0)
    g1 = send(g1, OVER)
    f3, g0, m = fence(send(f3, HOME), g0, m)
    f2 = plus(f2, f3)
    f2, g1 = fence(send(f2, HOME), g1)
    f1, g0 = fence(send(plus(f1, f2, g1), HOME), send(g0, ACROSS))
    proj = m.astype(F32) + f1[:n].astype(F32) + g0.astype(F32) + send(f1[n:], CORE).astype(F32)
    gate = lax.dynamic_index_in_dim(out_gate, levels[span], 0, keepdims=True)
    return (states.astype(F32) + gate * proj).astype(BF16)


def solution(mesh):
    return jax.shard_map(
        shards,
        mesh=mesh,
        in_specs=(
            P(("section", "head"), None),
            P(),
            P("section", None),
            P(),
            P(),
            P(None, "head"),
            P(None, "head"),
            P(None, "head"),
            P("head", None),
        ),
        out_specs=P(("section", "head"), None),
        check_vma=False,
    )
```
